32 devices in a mesh: dp: 8 (over y, x, core), et: 4 (over z).
Axes of the slice: x: 2, y: 2, z: 4, core: 2. Of those that a mesh axis runs over, the one named last changes fastest.
Arguments:
- out_grad: bfloat16 [4096, 4096], P(('dp', 'et')), may hold values from -6 to 6
- routes: int32 [4096, 2], P(('dp', 'et')), may hold values from 0 to 7, as said below
- gates: float32 [4096, 2], P(('dp', 'et')), may hold values from 0.05 to 1
- lengths: int32 [32, 8], P(('dp', 'et')), may hold values from 1 to 48, 128 in all within a row
- saved_gate: bfloat16 [8, 128, 16384], P('dp', None, 'et'), may hold values from -6 to 6
- saved_up: bfloat16 [8, 128, 16384], P('dp', None, 'et'), may hold values from -6 to 6
- w_gate: bfloat16 [4096, 16384], P('dp', 'et'), may hold values from -0.09375 to 0.09375
- w_up: bfloat16 [4096, 16384], P('dp', 'et'), may hold values from -0.09375 to 0.09375
- w_down: bfloat16 [16384, 4096], P('et', 'dp'), may hold values from -0.046875 to 0.046875
Outputs:
- input_grad: bfloat16 [4096, 4096], P(('dp', 'et'))
The draws below stay inside these ranges and needn't reach their ends.
Inputs may be any that keep to these rules, and one draw needn't show every extreme that they name: `routes`: the two ids of a row differ. In each block of 128 rows (one device's tokens) at most 32 rows name expert 0, and in every draw some block has exactly 32 of them.
All inputs are finite; a program needn't handle non-finite values.
Results may differ from the reference program's by a relative error of at most 0.0095.
Values may be sent and summed in bfloat16 or wider, within the bound.
No kernel may reach another device: no remote copies, remote signals or barrier semaphores. Data moves between devices by JAX's collectives and lax.ppermute only.
A program may use at most 256 MiB of HBM per device.

```python
import math
import jax
import jax.numpy as jnp
import numpy as np
from jax import lax

D = 4096
FF = 16384
EXPERTS = 8
TOK_DEV = 128
SEQS = 8
MOST_LEN = 48
CAP = 32
TOKENS = 4096
N_DP = 8
N_ET = 4
DEVICES = 32


def draw_routes(key, part):
    key = jax.random.fold_in(key, 11)
    blocks = TOKENS // TOK_DEV
    key_count, key_full, key_rank, key_second, key_first, key_offset, key_which = jax.random.split(key, 7)
    counts = jax.random.randint(key_count, (blocks,), CAP // 4, CAP + 1)
    full_block = jax.random.randint(key_full, (), 0, blocks)
    counts = jnp.where(jnp.arange(blocks) == full_block, CAP, counts)
    ranking = jax.vmap(lambda single: jax.random.permutation(single, TOK_DEV))(jax.random.split(key_rank, blocks))
    chosen = ranking < counts[:, None]
    second_id = jax.random.randint(key_second, (blocks, TOK_DEV), 1, EXPERTS)
    first_id = jax.random.randint(key_first, (blocks, TOK_DEV), 1, EXPERTS)
    offset = jax.random.randint(key_offset, (blocks, TOK_DEV), 1, EXPERTS - 1)
    other_id = 1 + (first_id - 1 + offset) % (EXPERTS - 1)
    which_first = jax.random.randint(key_which, (blocks, TOK_DEV), 0, 2)
    slot_one = jnp.where(chosen, jnp.where(which_first == 0, 0, second_id), first_id)
    slot_two = jnp.where(chosen, jnp.where(which_first == 0, second_id, 0), other_id)
    return jnp.stack([slot_one, slot_two], axis=-1).reshape(TOKENS, 2).astype(jnp.int32)


def block_scale(key, dims, cuts, smallest, high):
    level = 1.0
    for dim, blocks in cuts:
        heights = jax.random.uniform(jax.random.fold_in(jax.random.fold_in(key, 6), dim), (blocks,), jnp.float32, smallest / len(cuts), high / len(cuts))
        level = level * jnp.repeat(jnp.exp(heights), dims[dim] // blocks).reshape((-1,) + (1,) * (len(dims) - 1 - dim))
    return level


def profile(amount, total, bound, lean):
    portions = [(1 << 20) // math.isqrt(grade ** lean) + 1 for grade in range(2, amount + 1)]
    surplus, given = total - bound - (amount - 1), [1] * (amount - 1)
    while surplus > 0:
        free = [i for i in range(amount - 1) if given[i] < bound]
        whole, remaining = sum([portions[i] for i in free]), surplus
        for i in free:
            addition = min(bound - given[i], max(1, remaining * portions[i] // whole), surplus)
            given[i] = given[i] + addition
            surplus = surplus - addition
    return np.array([bound] + given)


def uneven(stream_key, count, total, reach, skew):
    if count == 2:
        one = jax.random.randint(stream_key, (), max(1, total - reach), min(reach, total - 1) + 1)
        return jnp.stack([one, total - one])
    tallies = jnp.asarray(profile(count, total, reach, skew), jnp.int32)
    twos = (count - 1) // 2
    donor, taker = tallies[1:1 + 2 * twos:2], tallies[2:2 + 2 * twos:2]
    margin = jnp.minimum(donor - 1, reach - taker)
    shifted = jax.random.randint(jax.random.fold_in(stream_key, 1), (twos,), 0, 1 << 20) % (margin + 1)
    tallies = tallies.at[1:1 + 2 * twos:2].set(donor - shifted).at[2:2 + 2 * twos:2].set(taker + shifted)
    return tallies[jax.random.permutation(jax.random.fold_in(stream_key, 2), count)]


def normal_values(own_key, dims, scale, bound, shards=(), kind=jnp.bfloat16):
    entries = jax.random.normal(own_key, dims, jnp.float32) * scale
    if len(shards) > 0:
        entries = block_scale(own_key, dims, shards, -0.22, 0.18) * entries
    return jnp.clip(entries, min=-bound, max=bound).astype(kind)


def setup_inputs(seed: int = 0) -> dict:
    key_of = jax.random.split(jax.random.key(seed), 10)
    return {
        "out_grad": normal_values(key_of[0], (TOKENS, D), 1.0, 6.0, ((0, 32),)),
        "routes": draw_routes(jax.random.fold_in(key_of[9], 71), 0),
        "gates": jnp.clip(0.05 + 0.95 * jax.random.uniform(key_of[2], (TOKENS, 2), jnp.float32) ** block_scale(key_of[2], (TOKENS, 2), ((0, 32),), -0.2, 0.2), 0.05, 1.0),
        "lengths": jax.vmap(lambda own: uneven(own, SEQS, TOK_DEV, MOST_LEN, 2))(jax.random.split(key_of[3], DEVICES)).reshape((DEVICES, SEQS)).astype(jnp.int32),
        "saved_gate": normal_values(key_of[4], (N_DP, N_ET * CAP, FF), 1.0, 6.0, ((0, 8), (2, 4))),
        "saved_up": normal_values(key_of[5], (N_DP, N_ET * CAP, FF), 1.0, 6.0, ((0, 8), (2, 4))),
        "w_gate": normal_values(key_of[6], (D, FF), D ** -0.5, 0.09375, ((0, 8), (1, 4))),
        "w_up": normal_values(key_of[7], (D, FF), D ** -0.5, 0.09375, ((0, 8), (1, 4))),
        "w_down": normal_values(key_of[8], (FF, D), FF ** -0.5, 0.046875, ((0, 4), (1, 8))),
    }


def reference(out_grad, routes, gates, lengths, saved_gate, saved_up, w_gate, w_up, w_down):
    hit_zero = routes == 0
    weight_zero = jnp.sum(jnp.where(hit_zero, gates, 0.0), axis=1)
    ends = jnp.cumsum(lengths, axis=1)
    starts = ends - lengths
    position = jnp.arange(TOK_DEV, dtype=jnp.int32)
    inside = (position[None, :, None] >= starts[:, None, :]) & (position[None, :, None] < ends[:, None, :])
    mean_len = TOK_DEV / SEQS
    factor = jnp.sum(jnp.where(inside, mean_len / lengths.astype(jnp.float32)[:, None, :], 0.0), axis=2).reshape(TOKENS)
    scaled = (out_grad.astype(jnp.float32) * (weight_zero * factor)[:, None]).astype(jnp.bfloat16)
    chosen = jnp.any(hit_zero, axis=1).reshape(N_DP * N_ET, TOK_DEV)
    slot_of = jnp.cumsum(chosen.astype(jnp.int32), axis=1) - 1
    placing = ((slot_of[:, None, :] == jnp.arange(CAP, dtype=jnp.int32)[None, :, None]) & chosen[:, None, :]).astype(jnp.float32)
    placing = placing.reshape(N_DP, N_ET, CAP, TOK_DEV)
    scaled_groups = scaled.reshape(N_DP, N_ET, TOK_DEV, D)
    hidden_dev = FF // N_ET
    gate_split = w_gate.astype(jnp.float32).reshape(D, N_ET, hidden_dev)
    up_split = w_up.astype(jnp.float32).reshape(D, N_ET, hidden_dev)
    down_full = w_down.astype(jnp.float32)

    def one_group(inputs):
        place_group, scaled_group, gate_group, up_group = inputs
        packed = jnp.einsum('jct,jtd->jcd', place_group, scaled_group.astype(jnp.float32)).reshape(N_ET * CAP, D)
        packed = packed.astype(jnp.bfloat16).astype(jnp.float32)
        upstream = jnp.einsum('rd,fd->rf', packed, down_full)
        gate_value = gate_group.astype(jnp.float32)
        up_value = up_group.astype(jnp.float32)
        sigmoid_gate = jax.nn.sigmoid(gate_value)
        slope = sigmoid_gate * (1.0 + gate_value * (1.0 - sigmoid_gate))
        grad_gate = (upstream * up_value * slope).astype(jnp.bfloat16)
        grad_up = (upstream * gate_value * sigmoid_gate).astype(jnp.bfloat16)
        grad_gate = grad_gate.astype(jnp.float32).reshape(N_ET * CAP, N_ET, hidden_dev)
        grad_up = grad_up.astype(jnp.float32).reshape(N_ET * CAP, N_ET, hidden_dev)
        partial_value = jnp.einsum('rsh,dsh->srd', grad_gate, gate_split) + jnp.einsum('rsh,dsh->srd', grad_up, up_split)
        rounded = lax.optimization_barrier(partial_value.astype(jnp.bfloat16))
        summed = jnp.sum(rounded.astype(jnp.float32), axis=0).astype(jnp.bfloat16)
        back = jnp.einsum('jct,jcd->jtd', place_group, summed.astype(jnp.float32).reshape(N_ET, CAP, D))
        return back.astype(jnp.bfloat16)

    result = lax.map(one_group, (placing, scaled_groups, saved_gate, saved_up))
    return result.reshape(TOKENS, D)
```

```python
import jax
import jax.numpy as jnp
from jax import lax
from jax.sharding import PartitionSpec as P


def swiglu_grads(upstream, gate_pre, up_pre):
    gate_value = gate_pre.astype(jnp.float32)
    up_value = up_pre.astype(jnp.float32)
    sigmoid_gate = jax.nn.sigmoid(gate_value)
    slope = sigmoid_gate * (1.0 + gate_value * (1.0 - sigmoid_gate))
    grad_gate = (upstream * up_value * slope).astype(jnp.bfloat16)
    grad_up = (upstream * gate_value * sigmoid_gate).astype(jnp.bfloat16)
    return (grad_gate, grad_up)


def contract_last(left, right):
    axis = left.ndim - 1
    return lax.dot_general(
        left, right, (((axis,), (1,)), ((), ())), preferred_element_type=jnp.float32
    )


def place_rows(routes, gates, lengths, slots):
    tok_rows = routes.shape[0]
    hit_zero = routes == 0
    weight_zero = jnp.sum(jnp.where(hit_zero, gates, 0.0), axis=1)
    chosen = jnp.any(hit_zero, axis=1)
    doc_len = lengths[0]
    ends = jnp.cumsum(doc_len)
    starts = ends - doc_len
    position = jnp.arange(tok_rows, dtype=jnp.int32)
    inside = (position[:, None] >= starts[None, :]) & (position[:, None] < ends[None, :])
    mean_len = tok_rows / doc_len.shape[0]
    factor = jnp.sum(
        jnp.where(inside, mean_len / doc_len.astype(jnp.float32)[None, :], 0.0), axis=1
    )
    slot_of = jnp.cumsum(chosen.astype(jnp.int32)) - 1
    placing = (
        (slot_of[None, :] == jnp.arange(slots, dtype=jnp.int32)[:, None]) & chosen[None, :]
    ).astype(jnp.bfloat16)
    return placing, weight_zero * factor


def per_device(out_grad, routes, gates, lengths, saved_gate, saved_up, w_gate, w_up, w_down):
    group_size = lax.axis_size("et")
    groups = lax.axis_size("dp")
    group_rows = saved_gate.shape[1]
    slots = group_rows // group_size
    width = w_gate.shape[0]
    placing, coef = place_rows(routes, gates, lengths, slots)
    scaled = (out_grad.astype(jnp.float32) * coef[:, None]).astype(jnp.bfloat16)
    packed = jnp.dot(placing, scaled, preferred_element_type=jnp.float32).astype(jnp.bfloat16)
    rows = lax.all_to_all(packed.reshape(slots, groups, width), "dp", split_axis=1, concat_axis=0)
    rows = rows.reshape(groups, slots, width)
    rows = lax.all_gather(rows, "et", axis=1)
    partial_up = contract_last(rows.reshape(groups * group_rows, width), w_down).astype(jnp.bfloat16)
    upstream = lax.psum_scatter(partial_up, "dp", scatter_dimension=0, tiled=True).astype(jnp.float32)
    grads = jnp.stack(swiglu_grads(upstream, saved_gate[0], saved_up[0]))
    grads = lax.all_gather(grads, "dp", axis=0)
    terms = contract_last(grads[:, 0], w_gate) + contract_last(grads[:, 1], w_up)
    terms = terms.astype(jnp.bfloat16).reshape(groups, group_size, slots, width)
    summed = lax.psum_scatter(terms, "et", scatter_dimension=1, tiled=False)
    summed = lax.all_to_all(summed, "dp", split_axis=0, concat_axis=1)
    summed = summed.reshape(slots, groups * width)
    input_grad = lax.dot_general(
        placing, summed, (((0,), (0,)), ((), ())), preferred_element_type=jnp.float32
    )
    return input_grad.astype(jnp.bfloat16)


def solution(mesh):
    in_specs = (
        P(("dp", "et"), None),
        P(("dp", "et"), None),
        P(("dp", "et"), None),
        P(("dp", "et"), None),
        P("dp", None, "et"),
        P("dp", None, "et"),
        P("dp", "et"),
        P("dp", "et"),
        P("et", "dp"),
    )
    out_specs = P(("dp", "et"), None)
    return jax.shard_map(
        per_device, mesh=mesh, in_specs=in_specs, out_specs=out_specs, check_vma=False
    )
```

```python
import jax
import jax.numpy as jnp
from jax import lax
from jax.sharding import PartitionSpec as P


def swiglu_grads(upstream, gate_pre, up_pre):
    gate_value = gate_pre.astype(jnp.float32)
    up_value = up_pre.astype(jnp.float32)
    sigmoid_gate = jax.nn.sigmoid(gate_value)
    slope = sigmoid_gate * (1.0 + gate_value * (1.0 - sigmoid_gate))
    grad_gate = (upstream * up_value * slope).astype(jnp.bfloat16)
    grad_up = (upstream * gate_value * sigmoid_gate).astype(jnp.bfloat16)
    return (grad_gate, grad_up)


def contract_last(left, right):
    axis = left.ndim - 1
    return lax.dot_general(
        left, right, (((axis,), (1,)), ((), ())), preferred_element_type=jnp.float32
    )


def place_rows(routes, gates, lengths, slots):
    tok_rows = routes.shape[0]
    hit_zero = routes == 0
    weight_zero = jnp.sum(jnp.where(hit_zero, gates, 0.0), axis=1)
    chosen = jnp.any(hit_zero, axis=1)
    doc_len = lengths[0]
    ends = jnp.cumsum(doc_len)
    starts = ends - doc_len
    position = jnp.arange(tok_rows, dtype=jnp.int32)
    inside = (position[:, None] >= starts[None, :]) & (position[:, None] < ends[None, :])
    mean_len = tok_rows / doc_len.shape[0]
    factor = jnp.sum(
        jnp.where(inside, mean_len / doc_len.astype(jnp.float32)[None, :], 0.0), axis=1
    )
    slot_of = jnp.cumsum(chosen.astype(jnp.int32)) - 1
    placing = (
        (slot_of[None, :] == jnp.arange(slots, dtype=jnp.int32)[:, None]) & chosen[None, :]
    ).astype(jnp.bfloat16)
    return placing, weight_zero * factor


def plain_exchange(out_grad, routes, gates, lengths, saved_gate, saved_up, w_gate, w_up, w_down):
    group_size = lax.axis_size("et")
    groups = lax.axis_size("dp")
    group_rows = saved_gate.shape[1]
    slots = group_rows // group_size
    width = w_gate.shape[0]
    placing, coef = place_rows(routes, gates, lengths, slots)
    scaled = (out_grad.astype(jnp.float32) * coef[:, None]).astype(jnp.bfloat16)
    packed = jnp.dot(placing, scaled, preferred_element_type=jnp.float32).astype(jnp.bfloat16)
    rows = lax.all_to_all(packed.reshape(slots, groups, width), "dp", split_axis=1, concat_axis=0)
    rows = rows.reshape(groups, slots, width)
    rows = lax.all_gather(rows, "et", axis=1)
    partial_up = contract_last(rows.reshape(groups * group_rows, width), w_down).astype(jnp.bfloat16)
    upstream = lax.psum_scatter(partial_up, "dp", scatter_dimension=0, tiled=True).astype(jnp.float32)
    grads = jnp.stack(swiglu_grads(upstream, saved_gate[0], saved_up[0]))
    grads = lax.all_gather(grads, "dp", axis=0)
    terms = contract_last(grads[:, 0], w_gate) + contract_last(grads[:, 1], w_up)
    terms = terms.astype(jnp.bfloat16).reshape(groups, group_size, slots, width)
    summed = lax.psum_scatter(terms, "et", scatter_dimension=1, tiled=False)
    summed = lax.all_to_all(summed, "dp", split_axis=0, concat_axis=1)
    summed = summed.reshape(slots, groups * width)
    input_grad = lax.dot_general(
        placing, summed, (((0,), (0,)), ((), ())), preferred_element_type=jnp.float32
    )
    return input_grad.astype(jnp.bfloat16)


def swap(values, axis, offset):
    size = lax.axis_size(axis)
    return lax.ppermute(values, axis, [(i, i ^ offset) for i in range(size)])


def scatter_sum(values, bits):
    for bit in bits:
        keep = [m for m in sorted(values) if not m & bit]
        sent = jnp.concatenate([values[m | bit] for m in keep], axis=0).astype(jnp.bfloat16)
        got = swap(sent, "dp", bit)
        rows = got.shape[0] // len(keep)
        values = {
            m: values[m].astype(jnp.float32) + got[i * rows : (i + 1) * rows].astype(jnp.float32)
            for i, m in enumerate(keep)
        }
    return values[0]


def gather_blocks(block, bits):
    order = [0]
    for bit in bits:
        block = jnp.concatenate([block, swap(block, "dp", bit)], axis=0)
        order = order + [m | bit for m in order]
    return block, order


def per_device(out_grad, routes, gates, lengths, saved_gate, saved_up, w_gate, w_up, w_down):
    planes = lax.axis_size("et")
    groups = lax.axis_size("dp")
    group_rows = saved_gate.shape[1]
    slots = group_rows // planes
    width, hidden = w_gate.shape
    half = hidden // 2
    quarter = half // 2
    me = lax.axis_index("dp")
    plane = lax.axis_index("et")
    core = me % 2
    mine, other = core * half, (1 - core) * half
    chip_bits = [1 << b for b in range(1, groups.bit_length() - 1)]
    orders = (chip_bits, chip_bits[::-1])
    chips = [2 * m for m in range(groups // 2)]

    placing, coef = place_rows(routes, gates, lengths, slots)
    scaled = (out_grad.astype(jnp.float32) * coef[:, None]).astype(jnp.bfloat16)
    packed = jnp.dot(placing, scaled, preferred_element_type=jnp.float32).astype(jnp.bfloat16)
    rows = lax.all_to_all(packed.reshape(slots, groups, width), "dp", split_axis=1, concat_axis=0)
    rows = rows.reshape(groups, slots, width)
    rows = jnp.take(rows, me ^ jnp.arange(groups), axis=0).reshape(groups * slots, width)

    down = jnp.concatenate(
        [
            lax.dynamic_slice_in_dim(w_down, mine, half, 0),
            swap(lax.dynamic_slice_in_dim(w_down, other, half, 0), "dp", 1),
        ],
        axis=1,
    )
    saved = jnp.stack([saved_gate[0], saved_up[0]])
    saved = jnp.stack(
        [
            lax.dynamic_slice_in_dim(saved, mine, half, 2),
            swap(lax.dynamic_slice_in_dim(saved, other, half, 2), "dp", 1),
        ],
        axis=1,
    ).reshape(2, 2, planes, slots, half)

    def hidden_part(weight, start):
        return lax.dynamic_slice_in_dim(weight, start, half, 1)

    ups = jnp.concatenate([hidden_part(w_gate, mine), hidden_part(w_up, mine)], axis=1)
    ups_sent = jnp.concatenate([hidden_part(w_gate, other), hidden_part(w_up, other)], axis=1)
    ups = jnp.concatenate([ups, swap(ups_sent, "dp", 1)], axis=0).reshape(2 * width, 2, 2, quarter)

    offsets = [0] + [s for s in range(2, planes)] + [1]
    total = None
    for offset in offsets:
        here = rows if offset == 0 else swap(rows, "et", offset)
        flipped = here.reshape(groups // 2, 2, slots, width)[:, ::-1].reshape(here.shape)
        here = jnp.concatenate([here, swap(flipped, "dp", 1)], axis=1)
        there = jnp.arange(2)
        saved_here = lax.dynamic_index_in_dim(saved, plane ^ offset, 2, keepdims=False)
        terms = None
        for part, bits in enumerate(orders):
            columns = slice(part * quarter, (part + 1) * quarter)
            partial_up = contract_last(here, down[columns]).astype(jnp.bfloat16)
            partial_up = partial_up.reshape(groups // 2, 2 * slots, quarter)
            upstream = scatter_sum({m: partial_up[m // 2] for m in chips}, bits)
            grads = jnp.concatenate(
                swiglu_grads(
                    upstream,
                    saved_here[0, :, :, columns].reshape(2 * slots, quarter),
                    saved_here[1, :, :, columns].reshape(2 * slots, quarter),
                ),
                axis=1,
            )
            grads, order = gather_blocks(grads, bits[::-1])
            grads = grads.reshape(groups // 2, 2 * slots, 2 * quarter)
            grads = jnp.stack([grads[order.index(m)] for m in chips])
            part_terms = contract_last(grads, ups[:, :, part].reshape(2 * width, 2 * quarter))
            terms = part_terms if terms is None else terms + part_terms
        terms = terms.reshape(groups // 2, 2, slots, 2, width)
        sent = terms[:, ::-1, :, 1].astype(jnp.bfloat16)
        terms = terms[:, :, :, 0] + swap(sent, "dp", 1).astype(jnp.float32)
        terms = terms.astype(jnp.bfloat16)
        if offset:
            terms = swap(terms, "et", offset)
        terms = terms.astype(jnp.float32)
        total = terms if total is None else total + terms
    summed = total.astype(jnp.bfloat16).reshape(groups, slots, width)
    summed = jnp.take(summed, me ^ jnp.arange(groups), axis=0)
    summed = lax.all_to_all(summed, "dp", split_axis=0, concat_axis=1)
    summed = summed.reshape(slots, groups * width)
    input_grad = lax.dot_general(
        placing, summed, (((0,), (0,)), ((), ())), preferred_element_type=jnp.float32
    )
    return input_grad.astype(jnp.bfloat16)


def solution(mesh):
    in_specs = (
        P(("dp", "et"), None),
        P(("dp", "et"), None),
        P(("dp", "et"), None),
        P(("dp", "et"), None),
        P("dp", None, "et"),
        P("dp", None, "et"),
        P("dp", "et"),
        P("dp", "et"),
        P("et", "dp"),
    )
    out_specs = P(("dp", "et"), None)
    body = per_device if mesh.shape["dp"] == 8 else plain_exchange
    return jax.shard_map(
        body, mesh=mesh, in_specs=in_specs, out_specs=out_specs, check_vma=False
    )
```

```python
import jax
import jax.numpy as jnp
from jax import lax
from jax.experimental import pallas as pl
from jax.experimental.pallas import tpu as pltpu
from jax.sharding import PartitionSpec as P


CHUNKS = (((0,), 0, 32), ((2,), 0, 32), ((3,), 0, 32), ((1,), 0, 32))
GATHERED = 4
ORDER = (
    (0, 0), (0, 1), (1, 0), (0, 2), (1, 1), (2, 0), (0, 3), (1, 2),
    (2, 1), (3, 0), (1, 3), (0, 4), (2, 2), (3, 1), (0, 5), (2, 3),
    (1, 4), (3, 2), (0, 6), (1, 5), (3, 3), (2, 4), (1, 6), (2, 5),
    (3, 4), (2, 6), (3, 5), (3, 6),
)


def swiglu_grads(upstream, gate_pre, up_pre):
    gate_value = gate_pre.astype(jnp.float32)
    up_value = up_pre.astype(jnp.float32)
    sigmoid_gate = jax.nn.sigmoid(gate_value)
    slope = sigmoid_gate * (1.0 + gate_value * (1.0 - sigmoid_gate))
    grad_gate = (upstream * up_value * slope).astype(jnp.bfloat16)
    grad_up = (upstream * gate_value * sigmoid_gate).astype(jnp.bfloat16)
    return (grad_gate, grad_up)


def contract_last(left, right):
    axis = left.ndim - 1
    return lax.dot_general(
        left, right, (((axis,), (1,)), ((), ())), preferred_element_type=jnp.float32
    )


def place_rows(routes, gates, lengths, slots):
    tok_rows = routes.shape[0]
    hit_zero = routes == 0
    weight_zero = jnp.sum(jnp.where(hit_zero, gates, 0.0), axis=1)
    chosen = jnp.any(hit_zero, axis=1)
    doc_len = lengths[0]
    ends = jnp.cumsum(doc_len)
    starts = ends - doc_len
    position = jnp.arange(tok_rows, dtype=jnp.int32)
    inside = (position[:, None] >= starts[None, :]) & (position[:, None] < ends[None, :])
    mean_len = tok_rows / doc_len.shape[0]
    factor = jnp.sum(
        jnp.where(inside, mean_len / doc_len.astype(jnp.float32)[None, :], 0.0), axis=1
    )
    slot_of = jnp.cumsum(chosen.astype(jnp.int32)) - 1
    placing = (
        (slot_of[None, :] == jnp.arange(slots, dtype=jnp.int32)[:, None]) & chosen[None, :]
    ).astype(jnp.bfloat16)
    return placing, weight_zero * factor


def plain_exchange(out_grad, routes, gates, lengths, saved_gate, saved_up, w_gate, w_up, w_down):
    group_size = lax.axis_size("et")
    groups = lax.axis_size("dp")
    group_rows = saved_gate.shape[1]
    slots = group_rows // group_size
    width = w_gate.shape[0]
    placing, coef = place_rows(routes, gates, lengths, slots)
    scaled = (out_grad.astype(jnp.float32) * coef[:, None]).astype(jnp.bfloat16)
    packed = jnp.dot(placing, scaled, preferred_element_type=jnp.float32).astype(jnp.bfloat16)
    rows = lax.all_to_all(packed.reshape(slots, groups, width), "dp", split_axis=1, concat_axis=0)
    rows = rows.reshape(groups, slots, width)
    rows = lax.all_gather(rows, "et", axis=1)
    partial_up = contract_last(rows.reshape(groups * group_rows, width), w_down).astype(jnp.bfloat16)
    upstream = lax.psum_scatter(partial_up, "dp", scatter_dimension=0, tiled=True).astype(jnp.float32)
    grads = jnp.stack(swiglu_grads(upstream, saved_gate[0], saved_up[0]))
    grads = lax.all_gather(grads, "dp", axis=0)
    terms = contract_last(grads[:, 0], w_gate) + contract_last(grads[:, 1], w_up)
    terms = terms.astype(jnp.bfloat16).reshape(groups, group_size, slots, width)
    summed = lax.psum_scatter(terms, "et", scatter_dimension=1, tiled=False)
    summed = lax.all_to_all(summed, "dp", split_axis=0, concat_axis=1)
    summed = summed.reshape(slots, groups * width)
    input_grad = lax.dot_general(
        placing, summed, (((0,), (0,)), ((), ())), preferred_element_type=jnp.float32
    )
    return input_grad.astype(jnp.bfloat16)


def swap(values, axis, offset):
    size = lax.axis_size(axis)
    return lax.ppermute(values, axis, [(i, i ^ offset) for i in range(size)])


def exchange(values, turn):
    size = lax.axis_size("dp")
    return lax.ppermute(values, "dp", [(i, i ^ (2 if (i + turn) % 2 == 0 else 4)) for i in range(size)])


def whole(array):
    return pl.BlockSpec(array.shape, lambda i, where: (0,) * len(array.shape))


def shape(rows, columns, kind=jnp.bfloat16):
    return jax.ShapeDtypeStruct((rows, columns), kind)


class Steps:
    def __init__(self, where):
        self.where = where
        self.last = []
        self.waits = []

    def call(self, kernel, out_shape, flops, moved, grid, in_specs, out_specs, operands, scratch_shapes=()):
        after = self.last + self.waits
        self.waits = []
        inputs = 1 + len(operands)

        def ordered(*refs):
            kernel(*refs[1:inputs], *refs[inputs + len(after) :])

        results = pl.pallas_call(
            ordered,
            out_shape=out_shape,
            cost_estimate=pl.CostEstimate(flops=flops, bytes_accessed=moved, transcendentals=0),
            compiler_params=pltpu.CompilerParams(vmem_limit_bytes=48 * 1024 * 1024),
            grid_spec=pltpu.PrefetchScalarGridSpec(
                num_scalar_prefetch=1,
                grid=grid,
                in_specs=list(in_specs) + [pl.BlockSpec(memory_space=pl.ANY)] * len(after),
                out_specs=out_specs,
                scratch_shapes=scratch_shapes,
            ),
        )(self.where, *operands, *after)
        self.last = list(results[:1])
        return results


def whole(array):
    return pl.BlockSpec(array.shape, lambda i, where: (0,) * len(array.shape))


def shape(rows, columns, kind=jnp.bfloat16):
    return jax.ShapeDtypeStruct((rows, columns), kind)


PARTNER_CHIP = (0, 2, 1, 3)


def partial_sums(steps, chunk, here, there, own_down, other_down, slots):
    offsets, low, high = chunk
    members, count = len(offsets), high - low
    width = own_down.shape[1]
    block = members * 2 * count
    half = own_down.shape[0] // 2
    step = half // 4

    def kernel(*refs):
        here_refs, there_refs = refs[:members], refs[members : 2 * members]
        own_ref, other_ref, send, keep, left = refs[2 * members :]

        @pl.when(pl.program_id(0) == 0)
        def _():
            for q in range(members):
                for chip in range(4):
                    for core in range(2):
                        to = chip * block + (q * 2 + core) * count
                        at = (chip * 2 + core) * slots + low
                        left[to : to + count, :width] = here_refs[q][0, at : at + count, :]
                        at = (PARTNER_CHIP[chip] * 2 + 1 - core) * slots + low
                        left[to : to + count, width:] = there_refs[q][0, at : at + count, :]

        sums = contract_last(left[:, :width], own_ref[...]) + contract_last(left[:, width:], other_ref[...])
        sums = sums.astype(jnp.bfloat16)
        keep[:block], send[:block] = sums[:block], sums[block : 2 * block]
        keep[block:], send[block:] = sums[2 * block : 3 * block], sums[3 * block :]

    weight = pl.BlockSpec((step, width), lambda i, where: (where[0] * 4 + i, 0))
    rows = here[0][0].shape[1]

    def row_spec(array, index):
        return pl.BlockSpec((1, rows, width), lambda i, where: (index(where), 0, 0))

    return steps.call(
        kernel,
        [shape(2 * block, half)] * 2,
        16 * block * width * half,
        4 * half * width + 8 * block * (2 * width + half),
        (4,),
        [row_spec(*x) for x in here + there] + [weight, weight],
        [pl.BlockSpec((2 * block, step), lambda i, where: (0, i))] * 2,
        [x[0] for x in here + there] + [own_down, other_down],
        [pltpu.VMEM((4 * block, 2 * width), jnp.bfloat16)],
    )


def second_terms(steps, keep, got):
    rows, columns = keep.shape[0] // 2, keep.shape[1]

    def kernel(keep, got, send):
        send[...] = (keep[...].astype(jnp.float32) + got[...].astype(jnp.float32)).astype(jnp.bfloat16)

    return steps.call(
        kernel,
        [shape(rows, columns)],
        rows * columns,
        6 * rows * columns,
        (1,),
        [pl.BlockSpec((rows, columns), lambda i, where: (1, 0))] * 2,
        [pl.BlockSpec((rows, columns), lambda i, where: (0, 0))],
        [keep, got],
    )[0]


def hidden_grads(steps, chunk, keep, got, last, saved):
    offsets, low, high = chunk
    members, count = len(offsets), high - low
    rows, columns = last.shape

    def kernel(keep, got, last, *refs):
        out = refs[-1]
        for q in range(members):
            for core in range(2):
                take = pl.ds((q * 2 + core) * count, count)
                upstream = (
                    keep[take, :].astype(jnp.float32)
                    + got[take, :].astype(jnp.float32)
                    + last[take, :].astype(jnp.float32)
                )
                gate, up = refs[(q * 2 + core) * 2 : (q * 2 + core) * 2 + 2]
                grad_gate, grad_up = swiglu_grads(upstream, gate[0], up[0])
                out[take, :columns] = grad_gate
                out[take, columns:] = grad_up

    upper = pl.BlockSpec((rows, columns), lambda i, where: (0, 0))
    slots = saved[0].shape[1] // lax.axis_size("et")

    def saved_spec(offset):
        return pl.BlockSpec(
            (1, count, columns),
            lambda i, where: (0, ((where[1] ^ offset) * slots + low) // count, where[0]),
        )

    return steps.call(
        kernel,
        [shape(rows, 2 * columns)],
        40 * rows * columns,
        14 * rows * columns,
        (1,),
        [upper] * 3 + [saved_spec(offset) for offset in offsets for _ in range(4)],
        [pl.BlockSpec((rows, 2 * columns), lambda i, where: (0, 0))],
        [keep, got, last] + saved * members,
    )[0]


def input_terms(steps, chunk, grads, weights):
    offsets, low, high = chunk
    members, count = len(offsets), high - low
    block, half = grads[0].shape[0], grads[0].shape[1] // 2
    rows = 4 * block
    width = weights[0].shape[0]
    step = width // 2

    def kernel(own, first_block, second_block, far_block, own_gate, own_up, other_gate, other_up, own_out, other_out, left):
        i = pl.program_id(0)

        @pl.when(i == 0)
        def _():
            for chip, source in enumerate((own, first_block, second_block, far_block)):
                left[chip * block : (chip + 1) * block, :] = source[...]

        def terms_of(gate, up):
            return contract_last(left[:, :half], gate[...]) + contract_last(left[:, half:], up[...])

        @pl.when(i < 2)
        def _():
            terms = terms_of(own_gate, own_up)
            for q in range(members):
                for chip in range(4):
                    to, at = (q * 4 + chip) * 2 * count, chip * block + q * 2 * count
                    own_out[to : to + 2 * count, :] = terms[at : at + 2 * count]

        @pl.when(i >= 2)
        def _():
            terms = terms_of(other_gate, other_up).astype(jnp.bfloat16)
            for q in range(members):
                for chip in range(4):
                    for core in range(2):
                        to = ((q * 4 + PARTNER_CHIP[chip]) * 2 + 1 - core) * count
                        at = chip * block + (q * 2 + core) * count
                        other_out[to : to + count, :] = terms[at : at + count]

    def first(i):
        return jnp.minimum(i, 1)

    def second(i):
        return jnp.maximum(i - 2, 0)

    own_weight = pl.BlockSpec((step, half), lambda i, where: (first(i), where[0]))
    other_weight = pl.BlockSpec((step, half), lambda i, where: (second(i), where[0]))
    return steps.call(
        kernel,
        [shape(rows, width, jnp.float32), shape(rows, width)],
        8 * rows * width * half,
        8 * width * half + 4 * rows * half + 6 * rows * width,
        (4,),
        [whole(x) for x in grads] + [own_weight] * 2 + [other_weight] * 2,
        [
            pl.BlockSpec((rows, step), lambda i, where: (0, first(i))),
            pl.BlockSpec((rows, step), lambda i, where: (0, second(i))),
        ],
        grads + weights,
        [pltpu.VMEM((rows, 2 * half), jnp.bfloat16)],
    )


def summed_terms(steps, own_terms, got, members):
    rows, width = own_terms.shape[0] // members, own_terms.shape[1]

    def kernel(own_terms, got, *outs):
        terms = (own_terms[...] + got[...].astype(jnp.float32)).astype(jnp.bfloat16)
        for q in range(members):
            outs[q][...] = terms[q * rows : (q + 1) * rows]

    return steps.call(
        kernel,
        [shape(rows, width)] * members,
        members * rows * width,
        8 * members * rows * width,
        (1,),
        [whole(own_terms), whole(got)],
        [pl.BlockSpec((rows, width), lambda i, where: (0, 0))] * members,
        [own_terms, got],
    )


def chunk_steps(steps, chunk, here, there, saved, weights, downs, slots):
    offsets, low, high = chunk
    send, keep = partial_sums(steps, chunk, here, there, *downs, slots)
    got = exchange(send, 0)
    yield
    last = exchange(second_terms(steps, keep, got), 1)
    yield
    own = hidden_grads(steps, chunk, keep, got, last, saved)
    from_second, from_first = exchange(own, 1), exchange(own, 0)
    yield
    far = exchange(from_second, 0)
    steps.waits = steps.waits + [from_second]
    yield
    own_terms, other_terms = input_terms(steps, chunk, [own, from_first, from_second, far], weights)
    got = swap(other_terms, "dp", 1)
    yield
    terms = summed_terms(steps, own_terms, got, len(offsets))
    terms = [part if offset == 0 else swap(part, "et", offset) for offset, part in zip(offsets, terms)]
    yield
    steps.waits = steps.waits + terms
    yield terms


def per_device(out_grad, routes, gates, lengths, saved_gate, saved_up, w_gate, w_up, w_down):
    planes = lax.axis_size("et")
    groups = lax.axis_size("dp")
    slots = saved_gate.shape[1] // planes
    width = w_gate.shape[0]
    me = lax.axis_index("dp")
    core = me % 2
    where = jnp.stack([core, lax.axis_index("et")]).astype(jnp.int32)

    downs = [w_down, swap(w_down, "dp", 1)]
    saved = [saved_gate, saved_up, swap(saved_gate, "dp", 1), swap(saved_up, "dp", 1)]
    weights = [w_gate, w_up, swap(w_gate, "dp", 1), swap(w_up, "dp", 1)]

    placing, coef = place_rows(routes, gates, lengths, slots)
    scaled = (out_grad.astype(jnp.float32) * coef[:, None]).astype(jnp.bfloat16)
    packed = jnp.dot(placing, scaled, preferred_element_type=jnp.float32).astype(jnp.bfloat16)
    rows = lax.all_to_all(packed.reshape(slots, groups, width), "dp", split_axis=1, concat_axis=0)
    rows = rows.reshape(groups, slots, width)
    chips = jnp.where(core == 0, jnp.array([0, 2, 4, 6]), jnp.array([0, 4, 2, 6]))
    place = me ^ (chips[:, None] + jnp.arange(2)[None, :]).reshape(groups)
    inverse = jnp.where(core == 0, jnp.arange(groups), jnp.array([0, 1, 4, 5, 2, 3, 6, 7]))
    inverse = jnp.take(inverse, me ^ jnp.arange(groups))
    rows = jnp.take(rows, place, axis=0).reshape(1, groups * slots, width)

    def here_index(offset):
        return lambda where: 0

    def plane_index(offset):
        return lambda where: where[1] ^ offset

    steps = Steps(where)
    sources, partners = {}, {}
    for offset in sorted({offset for offsets, _, _ in CHUNKS for offset in offsets}):
        if offset < GATHERED:
            source = rows if offset == 0 else swap(rows, "et", offset)
            sources[offset] = (source, here_index(offset))
            partners[offset] = (swap(source, "dp", 1), here_index(offset))
    if GATHERED < planes:
        gathered = lax.all_gather(rows, "et", axis=0, tiled=True)
        gathered_partner = swap(gathered, "dp", 1)
        for offset in range(GATHERED, planes):
            sources[offset] = (gathered, plane_index(offset))
            partners[offset] = (gathered_partner, plane_index(offset))
    chunks = [
        chunk_steps(
            steps,
            chunk,
            [sources[offset] for offset in chunk[0]],
            [partners[offset] for offset in chunk[0]],
            saved,
            weights,
            downs,
            slots,
        )
        for chunk in CHUNKS
    ]
    steps.waits = saved[2:] + weights[2:]
    parts = {}
    for k, _ in ORDER:
        for offset, part in zip(CHUNKS[k][0], next(chunks[k]) or []):
            parts.setdefault(offset, []).append(part.reshape(groups, -1, width))
    total = sum(jnp.concatenate(part, axis=1).astype(jnp.float32) for part in parts.values())
    summed = total.astype(jnp.bfloat16)
    summed = jnp.take(summed, inverse, axis=0)
    summed = lax.all_to_all(summed, "dp", split_axis=0, concat_axis=1)
    summed = summed.reshape(slots, groups * width)
    input_grad = lax.dot_general(
        placing, summed, (((0,), (0,)), ((), ())), preferred_element_type=jnp.float32
    )
    return input_grad.astype(jnp.bfloat16)


def solution(mesh):
    in_specs = (
        P(("dp", "et"), None),
        P(("dp", "et"), None),
        P(("dp", "et"), None),
        P(("dp", "et"), None),
        P("dp", None, "et"),
        P("dp", None, "et"),
        P("dp", "et"),
        P("dp", "et"),
        P("et", "dp"),
    )
    out_specs = P(("dp", "et"), None)
    body = per_device if mesh.shape["dp"] == 8 and mesh.shape["et"] == 4 else plain_exchange
    return jax.shard_map(
        body, mesh=mesh, in_specs=in_specs, out_specs=out_specs, check_vma=False
    )
```

```python
import jax
import jax.numpy as jnp
from jax import lax
from jax.experimental import pallas as pl
from jax.experimental.pallas import tpu as pltpu
from jax.sharding import PartitionSpec as P


VMEM_LIMIT = 24*1024*1024
PACK_LIMIT = 60 * 1024 * 1024
CHUNKS = (((0,), 0, 32), ((2,), 0, 32), ((3,), 0, 32), ((1,), 0, 32))
K1_STEPS = 4
K1_LIMIT = None
ORDER = (0, 1, -1, 0, 1, 0, 2, 2, 1, 0, 3, 1, 2, 3, 1, 0, 2, 3, 0, 2, 1, 3, 0, 1, 3, 2, 1, 2, 3, 2, 3, 3)


def swiglu_grads(upstream, gate_pre, up_pre):
    gate_value = gate_pre.astype(jnp.float32)
    up_value = up_pre.astype(jnp.float32)
    sigmoid_gate = jax.nn.sigmoid(gate_value)
    slope = sigmoid_gate * (1.0 + gate_value * (1.0 - sigmoid_gate))
    grad_gate = (upstream * up_value * slope).astype(jnp.bfloat16)
    grad_up = (upstream * gate_value * sigmoid_gate).astype(jnp.bfloat16)
    return (grad_gate, grad_up)


def contract_last(left, right):
    axis = left.ndim - 1
    return lax.dot_general(
        left, right, (((axis,), (1,)), ((), ())), preferred_element_type=jnp.float32
    )


def place_rows(routes, gates, lengths, slots):
    tok_rows = routes.shape[0]
    hit_zero = routes == 0
    weight_zero = jnp.sum(jnp.where(hit_zero, gates, 0.0), axis=1)
    chosen = jnp.any(hit_zero, axis=1)
    doc_len = lengths[0]
    ends = jnp.cumsum(doc_len)
    starts = ends - doc_len
    position = jnp.arange(tok_rows, dtype=jnp.int32)
    inside = (position[:, None] >= starts[None, :]) & (position[:, None] < ends[None, :])
    mean_len = tok_rows / doc_len.shape[0]
    factor = jnp.sum(
        jnp.where(inside, mean_len / doc_len.astype(jnp.float32)[None, :], 0.0), axis=1
    )
    slot_of = jnp.cumsum(chosen.astype(jnp.int32)) - 1
    placing = (
        (slot_of[None, :] == jnp.arange(slots, dtype=jnp.int32)[:, None]) & chosen[None, :]
    ).astype(jnp.bfloat16)
    return placing, weight_zero * factor


def plain_exchange(out_grad, routes, gates, lengths, saved_gate, saved_up, w_gate, w_up, w_down):
    group_size = lax.axis_size("et")
    groups = lax.axis_size("dp")
    group_rows = saved_gate.shape[1]
    slots = group_rows // group_size
    width = w_gate.shape[0]
    placing, coef = place_rows(routes, gates, lengths, slots)
    scaled = (out_grad.astype(jnp.float32) * coef[:, None]).astype(jnp.bfloat16)
    packed = jnp.dot(placing, scaled, preferred_element_type=jnp.float32).astype(jnp.bfloat16)
    rows = lax.all_to_all(packed.reshape(slots, groups, width), "dp", split_axis=1, concat_axis=0)
    rows = rows.reshape(groups, slots, width)
    rows = lax.all_gather(rows, "et", axis=1)
    partial_up = contract_last(rows.reshape(groups * group_rows, width), w_down).astype(jnp.bfloat16)
    upstream = lax.psum_scatter(partial_up, "dp", scatter_dimension=0, tiled=True).astype(jnp.float32)
    grads = jnp.stack(swiglu_grads(upstream, saved_gate[0], saved_up[0]))
    grads = lax.all_gather(grads, "dp", axis=0)
    terms = contract_last(grads[:, 0], w_gate) + contract_last(grads[:, 1], w_up)
    terms = terms.astype(jnp.bfloat16).reshape(groups, group_size, slots, width)
    summed = lax.psum_scatter(terms, "et", scatter_dimension=1, tiled=False)
    summed = lax.all_to_all(summed, "dp", split_axis=0, concat_axis=1)
    summed = summed.reshape(slots, groups * width)
    input_grad = lax.dot_general(
        placing, summed, (((0,), (0,)), ((), ())), preferred_element_type=jnp.float32
    )
    return input_grad.astype(jnp.bfloat16)


def swap(values, axis, offset):
    size = lax.axis_size(axis)
    return lax.ppermute(values, axis, [(i, i ^ offset) for i in range(size)])


def exchange(values, turn):
    size = lax.axis_size("dp")
    return lax.ppermute(values, "dp", [(i, i ^ (2 if (i + turn) % 2 == 0 else 4)) for i in range(size)])


def whole(array):
    return pl.BlockSpec(array.shape, lambda i, where: (0,) * len(array.shape))


def shape(rows, columns, kind=jnp.bfloat16):
    return jax.ShapeDtypeStruct((rows, columns), kind)


class Steps:
    def __init__(self, where):
        self.where = where
        self.last = []
        self.waits = []

    def call(self, kernel, out_shape, flops, moved, grid, in_specs, out_specs, operands, scratch_shapes=(), limit=None):
        after = self.last + self.waits
        self.waits = []
        inputs = 1 + len(operands)

        def ordered(*refs):
            kernel(*refs[:inputs], *refs[inputs + len(after) :])

        results = pl.pallas_call(
            ordered,
            out_shape=out_shape,
            cost_estimate=pl.CostEstimate(flops=flops, bytes_accessed=moved, transcendentals=0),
            compiler_params=pltpu.CompilerParams(vmem_limit_bytes=limit or VMEM_LIMIT),
            grid_spec=pltpu.PrefetchScalarGridSpec(
                num_scalar_prefetch=1,
                grid=grid,
                in_specs=list(in_specs) + [pl.BlockSpec(memory_space=pl.ANY)] * len(after),
                out_specs=out_specs,
                scratch_shapes=scratch_shapes,
            ),
        )(self.where, *operands, *after)
        self.last = list(results[:1])
        return results


def whole(array):
    return pl.BlockSpec(array.shape, lambda i, where: (0,) * len(array.shape))


def shape(rows, columns, kind=jnp.bfloat16):
    return jax.ShapeDtypeStruct((rows, columns), kind)


def packed_rows(steps, out_grad, routes, gates, lengths, groups, slots):
    tokens, columns = out_grad.shape
    width = columns // groups
    documents = lengths.shape[1]
    strips = 2
    each = groups // strips

    def kernel(where, grad_ref, routes_ref, gates_ref, lengths_ref, rows_ref, placing_ref, coef_ref):
        @pl.when(pl.program_id(0) == 0)
        def _():
            hit_zero = routes_ref[...] == 0
            weight_zero = jnp.sum(jnp.where(hit_zero, gates_ref[...], 0.0), axis=0, keepdims=True)
            chosen = jnp.sum(jnp.where(hit_zero, 1.0, 0.0), axis=0, keepdims=True)
            position = lax.broadcasted_iota(jnp.int32, (1, tokens), 1)
            own_len = jnp.ones((1, tokens), jnp.float32)
            start = 0
            for document in range(documents):
                length = lengths_ref[0, document]
                inside = (position >= start) & (position < start + length)
                own_len = jnp.where(inside, length.astype(jnp.float32), own_len)
                start = start + length
            coef = weight_zero * ((tokens / documents) / own_len)
            token = lax.broadcasted_iota(jnp.int32, (tokens, tokens), 0)
            earlier = jnp.where(token <= lax.broadcasted_iota(jnp.int32, (tokens, tokens), 1), 1.0, 0.0).astype(jnp.bfloat16)
            counts = jnp.dot(
                jnp.broadcast_to(chosen, (slots, tokens)).astype(jnp.bfloat16),
                earlier,
                preferred_element_type=jnp.float32,
            )
            slot = lax.broadcasted_iota(jnp.int32, (slots, tokens), 0)
            taken = (counts.astype(jnp.int32) - 1 == slot) & (chosen > 0.0)
            placing_ref[...] = jnp.where(taken, 1.0, 0.0).astype(jnp.bfloat16)
            coef_ref[...] = jnp.sum(jnp.where(taken, coef, 0.0), axis=1, keepdims=True)

        rows = jnp.dot(placing_ref[...], grad_ref[...], preferred_element_type=jnp.float32)
        rows = (rows * coef_ref[...]).astype(jnp.bfloat16)
        for k in range(each):
            rows_ref[k] = rows[:, k * width : (k + 1) * width]

    return steps.call(
        kernel,
        [jax.ShapeDtypeStruct((groups, slots, width), jnp.bfloat16), shape(slots, tokens)],
        2 * tokens * slots * columns,
        2 * tokens * columns + 2 * slots * columns,
        (strips,),
        [
            pl.BlockSpec((tokens, columns // strips), lambda i, where: (0, i)),
            whole(routes),
            whole(gates),
            pl.BlockSpec(memory_space=pltpu.SMEM),
        ],
        [
            pl.BlockSpec((each, slots, width), lambda i, where: (i, 0, 0)),
            pl.BlockSpec((slots, tokens), lambda i, where: (0, 0)),
        ],
        [out_grad, routes, gates, lengths],
        [pltpu.VMEM((slots, 1), jnp.float32)],
        PACK_LIMIT,
    )


def other_halves(steps, weights, saved):
    width, hidden = weights[0].shape
    rows = saved[0].shape[1]
    half = hidden // 2
    parts = 4

    def kernel(where, gate, up, saved_gate, saved_up, weights_out, saved_out):
        weights_out[0], weights_out[1] = gate[...], up[...]
        saved_out[0], saved_out[1] = saved_gate[0], saved_up[0]

    return steps.call(
        kernel,
        [
            jax.ShapeDtypeStruct((2, width, half), jnp.bfloat16),
            jax.ShapeDtypeStruct((2, rows, half), jnp.bfloat16),
        ],
        0,
        8 * (width + rows) * half,
        (parts,),
        [pl.BlockSpec((width // parts, half), lambda i, where: (i, 1 - where[0]))] * 2
        + [pl.BlockSpec((1, rows // parts, half), lambda i, where: (0, i, 1 - where[0]))] * 2,
        [
            pl.BlockSpec((2, width // parts, half), lambda i, where: (0, i, 0)),
            pl.BlockSpec((2, rows // parts, half), lambda i, where: (0, i, 0)),
        ],
        weights + saved,
    )


def arrived(steps, rows):
    def kernel(where, rows, out):
        out[...] = rows[...]

    return steps.call(
        kernel,
        [jax.ShapeDtypeStruct(rows.shape, rows.dtype)],
        0,
        4 * rows.size,
        (1,),
        [whole(rows)],
        [whole(rows)],
        [rows],
    )[0]


def partial_sums(steps, chunk, here, there, own_down, other_down):
    offsets, low, high = chunk
    members, count = len(offsets), high - low
    width = own_down.shape[1]
    block = members * 2 * count
    half = own_down.shape[0] // 2
    step = half // K1_STEPS

    def kernel(where, *refs):
        own_ref, other_ref, send, keep, left = refs[2 * members :]

        @pl.when(pl.program_id(0) == 0)
        def _():
            for q in range(members):
                for place in range(8):
                    to = place // 2 * block + (q * 2 + place % 2) * count
                    group = where[2 + place]
                    left[to : to + count, :width] = refs[q][group, low:high, :]
                    left[to : to + count, width:] = refs[members + q][group, low:high, :]

        sums = contract_last(left[:, :width], own_ref[...]) + contract_last(left[:, width:], other_ref[...])
        sums = sums.astype(jnp.bfloat16)
        keep[:block], send[:block] = sums[:block], sums[block : 2 * block]
        keep[block:], send[block:] = sums[2 * block : 3 * block], sums[3 * block :]

    weight = pl.BlockSpec((step, width), lambda i, where: (where[0] * K1_STEPS + i, 0))
    return steps.call(
        kernel,
        [shape(2 * block, half)] * 2,
        16 * block * width * half,
        4 * half * width + 8 * block * (2 * width + half),
        (K1_STEPS,),
        [whole(x) for x in here + there] + [weight, weight],
        [pl.BlockSpec((2 * block, step), lambda i, where: (0, i))] * 2,
        here + there + [own_down, other_down],
        [pltpu.VMEM((4 * block, 2 * width), jnp.bfloat16)],
        K1_LIMIT,
    )


def second_terms(steps, keep, got):
    rows, columns = keep.shape[0] // 2, keep.shape[1]

    def kernel(where, keep, got, send):
        send[...] = (keep[...].astype(jnp.float32) + got[...].astype(jnp.float32)).astype(jnp.bfloat16)

    return steps.call(
        kernel,
        [shape(rows, columns)],
        rows * columns,
        6 * rows * columns,
        (1,),
        [pl.BlockSpec((rows, columns), lambda i, where: (1, 0))] * 2,
        [pl.BlockSpec((rows, columns), lambda i, where: (0, 0))],
        [keep, got],
    )[0]


def hidden_grads(steps, chunk, keep, got, last, saved):
    offsets, low, high = chunk
    members, count = len(offsets), high - low
    rows, columns = last.shape

    def kernel(where, keep, got, last, *refs):
        out = refs[-1]
        for q in range(members):
            for core in range(2):
                take = pl.ds((q * 2 + core) * count, count)
                upstream = (
                    keep[take, :].astype(jnp.float32)
                    + got[take, :].astype(jnp.float32)
                    + last[take, :].astype(jnp.float32)
                )
                gate, up = refs[(q * 2 + core) * 2 : (q * 2 + core) * 2 + 2]
                grad_gate, grad_up = swiglu_grads(upstream, gate[0], up[0])
                out[take, :columns] = grad_gate
                out[take, columns:] = grad_up

    upper = pl.BlockSpec((rows, columns), lambda i, where: (0, 0))
    slots = saved[0].shape[1] // lax.axis_size("et")

    def row(where, offset):
        return ((where[1] ^ offset) * slots + low) // count

    def own_spec(offset):
        return pl.BlockSpec((1, count, columns), lambda i, where: (0, row(where, offset), where[0]))

    def other_spec(offset, which):
        return pl.BlockSpec((1, count, columns), lambda i, where: (which, row(where, offset), 0))

    saved_specs = [
        spec for offset in offsets for spec in [own_spec(offset)] * 2 + [other_spec(offset, k) for k in range(2)]
    ]
    return steps.call(
        kernel,
        [shape(rows, 2 * columns)],
        40 * rows * columns,
        14 * rows * columns,
        (1,),
        [upper] * 3 + saved_specs,
        [pl.BlockSpec((rows, 2 * columns), lambda i, where: (0, 0))],
        [keep, got, last] + (saved[:2] + [saved[2]] * 2) * members,
    )[0]


def input_terms(steps, chunk, grads, weights):
    offsets, low, high = chunk
    members, count = len(offsets), high - low
    block, half = grads[0].shape[0], grads[0].shape[1] // 2
    rows = 4 * block
    width = weights[0].shape[0]
    step = width // 2

    def kernel(where, own, first_block, second_block, far_block, own_gate, own_up, other_gate, other_up, *refs):
        own_out, other_out, left = refs
        i = pl.program_id(0)

        @pl.when(i == 0)
        def _():
            for chip, source in enumerate((own, first_block, second_block, far_block)):
                left[chip * block : (chip + 1) * block, :] = source[...]

        def terms_of(gate, up):
            return contract_last(left[:, :half], gate) + contract_last(left[:, half:], up)

        @pl.when(i < 2)
        def _():
            terms = terms_of(own_gate[...], own_up[...])
            for q in range(members):
                for place in range(8):
                    at = place // 2 * block + (q * 2 + place % 2) * count
                    own_out[q, where[2 + place]] = terms[at : at + count]

        @pl.when(i >= 2)
        def _():
            terms = terms_of(other_gate[0], other_up[0]).astype(jnp.bfloat16)
            for q in range(members):
                for place in range(8):
                    at = place // 2 * block + (q * 2 + place % 2) * count
                    other_out[q, where[2 + place]] = terms[at : at + count]

    def first(i):
        return jnp.minimum(i, 1)

    def second(i):
        return jnp.maximum(i - 2, 0)

    own_weight = pl.BlockSpec((step, half), lambda i, where: (first(i), where[0]))
    other_weights = [
        pl.BlockSpec((1, step, half), lambda i, where, k=k: (k, second(i), 0)) for k in range(2)
    ]
    return steps.call(
        kernel,
        [
            jax.ShapeDtypeStruct((members, 8, count, width), jnp.float32),
            jax.ShapeDtypeStruct((members, 8, count, width), jnp.bfloat16),
        ],
        8 * rows * width * half,
        8 * width * half + 4 * rows * half + 6 * rows * width,
        (4,),
        [whole(x) for x in grads] + [own_weight] * 2 + other_weights,
        [
            pl.BlockSpec((members, 8, count, step), lambda i, where: (0, 0, 0, first(i))),
            pl.BlockSpec((members, 8, count, step), lambda i, where: (0, 0, 0, second(i))),
        ],
        grads + weights[:2] + [weights[2]] * 2,
        [pltpu.VMEM((rows, 2 * half), jnp.bfloat16)],
    )


def summed_terms(steps, own_terms, got):
    members, *rest = own_terms.shape

    def kernel(where, own_terms, got, *outs):
        for q in range(members):
            outs[q][...] = (own_terms[q] + got[q].astype(jnp.float32)).astype(jnp.bfloat16)

    return steps.call(
        kernel,
        [jax.ShapeDtypeStruct(rest, jnp.bfloat16)] * members,
        own_terms.size,
        8 * own_terms.size,
        (1,),
        [whole(own_terms), whole(got)],
        [pl.BlockSpec(rest, lambda i, where: (0, 0, 0))] * members,
        [own_terms, got],
    )


def chunk_steps(steps, chunk, here, saved, weights, downs):
    offsets, low, high = chunk
    if any(offsets):
        here = [arrived(steps, x) for x in here]
        yield
    there = [swap(x, "dp", 1) for x in here]
    send, keep = partial_sums(steps, chunk, here, there, *downs)
    got = exchange(send, 0)
    yield
    last = exchange(second_terms(steps, keep, got), 1)
    yield
    own = hidden_grads(steps, chunk, keep, got, last, saved)
    from_second, from_first = exchange(own, 1), exchange(own, 0)
    yield
    far = exchange(from_second, 0)
    steps.waits = steps.waits + [from_second]
    yield
    own_terms, other_terms = input_terms(steps, chunk, [own, from_first, from_second, far], weights)
    got = swap(other_terms, "dp", 1)
    yield
    terms = summed_terms(steps, own_terms, got)
    terms = [part if offset == 0 else swap(part, "et", offset) for offset, part in zip(offsets, terms)]
    yield
    steps.waits = steps.waits + terms
    yield terms


def per_device(out_grad, routes, gates, lengths, saved_gate, saved_up, w_gate, w_up, w_down):
    groups = lax.axis_size("dp")
    slots = saved_gate.shape[1] // lax.axis_size("et")
    width = w_gate.shape[0]
    me = lax.axis_index("dp")
    core = me % 2
    first, second = 2 + 2 * core, 4 - 2 * core
    place = [me ^ (chip + pair) for chip in (0, first, second, 6) for pair in (0, 1)]
    where = jnp.stack([core, lax.axis_index("et")] + place).astype(jnp.int32)

    downs = [w_down, swap(w_down, "dp", 1)]
    saved = [saved_gate, saved_up]
    weights = [w_gate, w_up]

    steps = Steps(where)
    rows, placing = packed_rows(steps, out_grad, routes.T, gates.T, lengths, groups, slots)
    rows = lax.all_to_all(rows, "dp", split_axis=0, concat_axis=0, tiled=True)
    sources = {
        offset: rows if offset == 0 else swap(rows, "et", offset)
        for offset in sorted({offset for offsets, _, _ in CHUNKS for offset in offsets})
    }
    chunks = [
        chunk_steps(steps, chunk, [sources[offset] for offset in chunk[0]], saved, weights, downs)
        for chunk in CHUNKS
    ]
    parts = {}
    steps.waits = [rows]
    for k in ORDER:
        if k < 0:
            other_weights, other_saved = other_halves(steps, weights, saved)
            weights.append(swap(other_weights, "dp", 1))
            saved.append(swap(other_saved, "dp", 1))
            continue
        for offset, part in zip(CHUNKS[k][0], next(chunks[k]) or []):
            parts.setdefault(offset, []).append(part)
    total = sum(jnp.concatenate(part, axis=1).astype(jnp.float32) for part in parts.values())
    summed = total.astype(jnp.bfloat16)
    summed = lax.all_to_all(summed, "dp", split_axis=0, concat_axis=1)
    summed = summed.reshape(slots, groups * width)
    input_grad = lax.dot_general(
        placing, summed, (((0,), (0,)), ((), ())), preferred_element_type=jnp.float32
    )
    return input_grad.astype(jnp.bfloat16)


def solution(mesh):
    in_specs = (
        P(("dp", "et"), None),
        P(("dp", "et"), None),
        P(("dp", "et"), None),
        P(("dp", "et"), None),
        P("dp", None, "et"),
        P("dp", None, "et"),
        P("dp", "et"),
        P("dp", "et"),
        P("et", "dp"),
    )
    out_specs = P(("dp", "et"), None)
    body = per_device if mesh.shape["dp"] == 8 and mesh.shape["et"] == 4 else plain_exchange
    return jax.shard_map(
        body, mesh=mesh, in_specs=in_specs, out_specs=out_specs, check_vma=False
    )
```

```python
import jax
import jax.numpy as jnp
from jax import lax
from jax.experimental import pallas as pl
from jax.experimental.pallas import tpu as pltpu
from jax.sharding import PartitionSpec as P


VMEM_LIMIT = 24 * 1024 * 1024
PACK_LIMIT = 60 * 1024 * 1024
CHUNKS = (((0,), 0, 32), ((2,), 0, 32), ((3,), 0, 32), ((1,), 0, 32))
SUM_STEPS = 4
ORDER = (0, 1, -1, 0, 1, 2, 0, 2, 0, 1, 3, 1, 2, 3, 1, 0, 2, 3, 0, 2, 3, 0, 1, 1, 3, 2, 1, 2, 3, 2, 3, 3)


def swiglu_grads(upstream, gate_pre, up_pre):
    gate_value = gate_pre.astype(jnp.float32)
    up_value = up_pre.astype(jnp.float32)
    sigmoid_gate = jax.nn.sigmoid(gate_value)
    slope = sigmoid_gate * (1.0 + gate_value * (1.0 - sigmoid_gate))
    grad_gate = (upstream * up_value * slope).astype(jnp.bfloat16)
    grad_up = (upstream * gate_value * sigmoid_gate).astype(jnp.bfloat16)
    return (grad_gate, grad_up)


def contract_last(left, right):
    axis = left.ndim - 1
    return lax.dot_general(
        left, right, (((axis,), (1,)), ((), ())), preferred_element_type=jnp.float32
    )


def place_rows(routes, gates, lengths, slots):
    tok_rows = routes.shape[0]
    hit_zero = routes == 0
    weight_zero = jnp.sum(jnp.where(hit_zero, gates, 0.0), axis=1)
    chosen = jnp.any(hit_zero, axis=1)
    doc_len = lengths[0]
    ends = jnp.cumsum(doc_len)
    starts = ends - doc_len
    position = jnp.arange(tok_rows, dtype=jnp.int32)
    inside = (position[:, None] >= starts[None, :]) & (position[:, None] < ends[None, :])
    mean_len = tok_rows / doc_len.shape[0]
    factor = jnp.sum(
        jnp.where(inside, mean_len / doc_len.astype(jnp.float32)[None, :], 0.0), axis=1
    )
    slot_of = jnp.cumsum(chosen.astype(jnp.int32)) - 1
    placing = (
        (slot_of[None, :] == jnp.arange(slots, dtype=jnp.int32)[:, None]) & chosen[None, :]
    ).astype(jnp.bfloat16)
    return placing, weight_zero * factor


def plain_exchange(out_grad, routes, gates, lengths, saved_gate, saved_up, w_gate, w_up, w_down):
    group_size = lax.axis_size("et")
    groups = lax.axis_size("dp")
    group_rows = saved_gate.shape[1]
    slots = group_rows // group_size
    width = w_gate.shape[0]
    placing, coef = place_rows(routes, gates, lengths, slots)
    scaled = (out_grad.astype(jnp.float32) * coef[:, None]).astype(jnp.bfloat16)
    packed = jnp.dot(placing, scaled, preferred_element_type=jnp.float32).astype(jnp.bfloat16)
    rows = lax.all_to_all(packed.reshape(slots, groups, width), "dp", split_axis=1, concat_axis=0)
    rows = rows.reshape(groups, slots, width)
    rows = lax.all_gather(rows, "et", axis=1)
    partial_up = contract_last(rows.reshape(groups * group_rows, width), w_down).astype(jnp.bfloat16)
    upstream = lax.psum_scatter(partial_up, "dp", scatter_dimension=0, tiled=True).astype(jnp.float32)
    grads = jnp.stack(swiglu_grads(upstream, saved_gate[0], saved_up[0]))
    grads = lax.all_gather(grads, "dp", axis=0)
    terms = contract_last(grads[:, 0], w_gate) + contract_last(grads[:, 1], w_up)
    terms = terms.astype(jnp.bfloat16).reshape(groups, group_size, slots, width)
    summed = lax.psum_scatter(terms, "et", scatter_dimension=1, tiled=False)
    summed = lax.all_to_all(summed, "dp", split_axis=0, concat_axis=1)
    summed = summed.reshape(slots, groups * width)
    input_grad = lax.dot_general(
        placing, summed, (((0,), (0,)), ((), ())), preferred_element_type=jnp.float32
    )
    return input_grad.astype(jnp.bfloat16)


def swap(values, axis, offset):
    size = lax.axis_size(axis)
    return lax.ppermute(values, axis, [(i, i ^ offset) for i in range(size)])


def exchange(values, turn):
    size = lax.axis_size("dp")
    return lax.ppermute(values, "dp", [(i, i ^ (2 if (i + turn) % 2 == 0 else 4)) for i in range(size)])


def whole(array):
    return pl.BlockSpec(array.shape, lambda i, where: (0,) * len(array.shape))


def shape(rows, columns, kind=jnp.bfloat16):
    return jax.ShapeDtypeStruct((rows, columns), kind)


class Steps:
    def __init__(self, where):
        self.where = where
        self.last = []
        self.waits = []

    def call(self, kernel, out_shape, flops, moved, grid, in_specs, out_specs, operands, scratch_shapes=(), limit=None, where=None):
        after = self.last + self.waits
        self.waits = []
        inputs = 1 + len(operands)

        def ordered(*refs):
            kernel(*refs[:inputs], *refs[inputs + len(after) :])

        results = pl.pallas_call(
            ordered,
            out_shape=out_shape,
            cost_estimate=pl.CostEstimate(flops=flops, bytes_accessed=moved, transcendentals=0),
            compiler_params=pltpu.CompilerParams(vmem_limit_bytes=limit or VMEM_LIMIT),
            grid_spec=pltpu.PrefetchScalarGridSpec(
                num_scalar_prefetch=1,
                grid=grid,
                in_specs=list(in_specs) + [pl.BlockSpec(memory_space=pl.ANY)] * len(after),
                out_specs=out_specs,
                scratch_shapes=scratch_shapes,
            ),
        )(self.where if where is None else where, *operands, *after)
        self.last = list(results[:1])
        return results


def whole(array):
    return pl.BlockSpec(array.shape, lambda i, where: (0,) * len(array.shape))


def shape(rows, columns, kind=jnp.bfloat16):
    return jax.ShapeDtypeStruct((rows, columns), kind)


def packed_rows(steps, out_grad, routes, gates, lengths, groups, slots):
    tokens, columns = out_grad.shape
    width = columns // groups
    documents = lengths.shape[1]
    strips = 2
    each = groups // strips

    def kernel(where, grad_ref, routes_ref, gates_ref, lengths_ref, rows_ref, placing_ref, coef_ref):
        @pl.when(pl.program_id(0) == 0)
        def _():
            hit_zero = routes_ref[...] == 0
            weight_zero = jnp.sum(jnp.where(hit_zero, gates_ref[...], 0.0), axis=0, keepdims=True)
            chosen = jnp.sum(jnp.where(hit_zero, 1.0, 0.0), axis=0, keepdims=True)
            position = lax.broadcasted_iota(jnp.int32, (1, tokens), 1)
            own_len = jnp.ones((1, tokens), jnp.float32)
            start = 0
            for document in range(documents):
                length = lengths_ref[0, document]
                inside = (position >= start) & (position < start + length)
                own_len = jnp.where(inside, length.astype(jnp.float32), own_len)
                start = start + length
            coef = weight_zero * ((tokens / documents) / own_len)
            token = lax.broadcasted_iota(jnp.int32, (tokens, tokens), 0)
            earlier = jnp.where(token <= lax.broadcasted_iota(jnp.int32, (tokens, tokens), 1), 1.0, 0.0).astype(jnp.bfloat16)
            counts = jnp.dot(
                jnp.broadcast_to(chosen, (slots, tokens)).astype(jnp.bfloat16),
                earlier,
                preferred_element_type=jnp.float32,
            )
            slot = lax.broadcasted_iota(jnp.int32, (slots, tokens), 0)
            taken = (counts.astype(jnp.int32) - 1 == slot) & (chosen > 0.0)
            placing_ref[...] = jnp.where(taken, 1.0, 0.0).astype(jnp.bfloat16)
            coef_ref[...] = jnp.sum(jnp.where(taken, coef, 0.0), axis=1, keepdims=True)

        rows = jnp.dot(placing_ref[...], grad_ref[...], preferred_element_type=jnp.float32)
        rows = (rows * coef_ref[...]).astype(jnp.bfloat16)
        for k in range(each):
            rows_ref[k] = rows[:, k * width : (k + 1) * width]

    return steps.call(
        kernel,
        [jax.ShapeDtypeStruct((groups, slots, width), jnp.bfloat16), shape(slots, tokens)],
        2 * tokens * slots * columns,
        2 * tokens * columns + 2 * slots * columns,
        (strips,),
        [
            pl.BlockSpec((tokens, columns // strips), lambda i, where: (0, i)),
            whole(routes),
            whole(gates),
            pl.BlockSpec(memory_space=pltpu.SMEM),
        ],
        [
            pl.BlockSpec((each, slots, width), lambda i, where: (i, 0, 0)),
            pl.BlockSpec((slots, tokens), lambda i, where: (0, 0)),
        ],
        [out_grad, routes, gates, lengths],
        [pltpu.VMEM((slots, 1), jnp.float32)],
        PACK_LIMIT,
        jnp.zeros((1,), jnp.int32),
    )


def other_halves(steps, weights, saved):
    width, hidden = weights[0].shape
    rows = saved[0].shape[1]
    half = hidden // 2
    parts = 4

    def kernel(where, gate, up, saved_gate, saved_up, weights_out, saved_out):
        weights_out[0], weights_out[1] = gate[...], up[...]
        saved_out[0], saved_out[1] = saved_gate[0], saved_up[0]

    return steps.call(
        kernel,
        [
            jax.ShapeDtypeStruct((2, width, half), jnp.bfloat16),
            jax.ShapeDtypeStruct((2, rows, half), jnp.bfloat16),
        ],
        0,
        8 * (width + rows) * half,
        (parts,),
        [pl.BlockSpec((width // parts, half), lambda i, where: (i, 1 - where[0]))] * 2
        + [pl.BlockSpec((1, rows // parts, half), lambda i, where: (0, i, 1 - where[0]))] * 2,
        [
            pl.BlockSpec((2, width // parts, half), lambda i, where: (0, i, 0)),
            pl.BlockSpec((2, rows // parts, half), lambda i, where: (0, i, 0)),
        ],
        weights + saved,
    )


def arrived(steps, rows):
    def kernel(where, rows, out):
        out[...] = rows[...]

    return steps.call(
        kernel,
        [jax.ShapeDtypeStruct(rows.shape, rows.dtype)],
        0,
        4 * rows.size,
        (1,),
        [whole(rows)],
        [whole(rows)],
        [rows],
    )[0]


def partial_sums(steps, chunk, here, there, own_down, other_down):
    offsets, low, high = chunk
    members, count = len(offsets), high - low
    width = own_down.shape[1]
    block = members * 2 * count
    half = own_down.shape[0] // 2
    step = half // SUM_STEPS

    def kernel(where, *refs):
        own_ref, other_ref, send, keep, left = refs[2 * members :]

        @pl.when(pl.program_id(0) == 0)
        def _():
            for q in range(members):
                for place in range(8):
                    to = place // 2 * block + (q * 2 + place % 2) * count
                    group = where[2 + place]
                    left[to : to + count, :width] = refs[q][group, low:high, :]
                    left[to : to + count, width:] = refs[members + q][group, low:high, :]

        sums = contract_last(left[:, :width], own_ref[...]) + contract_last(left[:, width:], other_ref[...])
        sums = sums.astype(jnp.bfloat16)
        keep[:block], send[:block] = sums[:block], sums[block : 2 * block]
        keep[block:], send[block:] = sums[2 * block : 3 * block], sums[3 * block :]

    weight = pl.BlockSpec((step, width), lambda i, where: (where[0] * SUM_STEPS + i, 0))
    return steps.call(
        kernel,
        [shape(2 * block, half)] * 2,
        16 * block * width * half,
        4 * half * width + 8 * block * (2 * width + half),
        (SUM_STEPS,),
        [whole(x) for x in here + there] + [weight, weight],
        [pl.BlockSpec((2 * block, step), lambda i, where: (0, i))] * 2,
        here + there + [own_down, other_down],
        [pltpu.VMEM((4 * block, 2 * width), jnp.bfloat16)],
    )


def second_terms(steps, keep, got):
    rows, columns = keep.shape[0] // 2, keep.shape[1]

    def kernel(where, keep, got, send):
        send[...] = (keep[...].astype(jnp.float32) + got[...].astype(jnp.float32)).astype(jnp.bfloat16)

    return steps.call(
        kernel,
        [shape(rows, columns)],
        rows * columns,
        6 * rows * columns,
        (1,),
        [pl.BlockSpec((rows, columns), lambda i, where: (1, 0))] * 2,
        [pl.BlockSpec((rows, columns), lambda i, where: (0, 0))],
        [keep, got],
    )[0]


def hidden_grads(steps, chunk, keep, got, last, saved):
    offsets, low, high = chunk
    members, count = len(offsets), high - low
    rows, columns = last.shape

    def kernel(where, keep, got, last, *refs):
        out = refs[-1]
        for q in range(members):
            for core in range(2):
                take = pl.ds((q * 2 + core) * count, count)
                upstream = (
                    keep[take, :].astype(jnp.float32)
                    + got[take, :].astype(jnp.float32)
                    + last[take, :].astype(jnp.float32)
                )
                gate, up = refs[(q * 2 + core) * 2 : (q * 2 + core) * 2 + 2]
                grad_gate, grad_up = swiglu_grads(upstream, gate[0], up[0])
                out[take, :columns] = grad_gate
                out[take, columns:] = grad_up

    upper = pl.BlockSpec((rows, columns), lambda i, where: (0, 0))
    slots = saved[0].shape[1] // lax.axis_size("et")

    def row(where, offset):
        return ((where[1] ^ offset) * slots + low) // count

    def own_spec(offset):
        return pl.BlockSpec((1, count, columns), lambda i, where: (0, row(where, offset), where[0]))

    def other_spec(offset, which):
        return pl.BlockSpec((1, count, columns), lambda i, where: (which, row(where, offset), 0))

    saved_specs = [
        spec for offset in offsets for spec in [own_spec(offset)] * 2 + [other_spec(offset, k) for k in range(2)]
    ]
    return steps.call(
        kernel,
        [shape(rows, 2 * columns)],
        40 * rows * columns,
        14 * rows * columns,
        (1,),
        [upper] * 3 + saved_specs,
        [pl.BlockSpec((rows, 2 * columns), lambda i, where: (0, 0))],
        [keep, got, last] + (saved[:2] + [saved[2]] * 2) * members,
    )[0]


def input_terms(steps, chunk, grads, weights):
    offsets, low, high = chunk
    members, count = len(offsets), high - low
    block, half = grads[0].shape[0], grads[0].shape[1] // 2
    rows = 4 * block
    width = weights[0].shape[0]
    step = width // 2

    def kernel(where, own, first_block, second_block, far_block, own_gate, own_up, other_gate, other_up, *refs):
        own_out, other_out, left = refs
        i = pl.program_id(0)

        @pl.when(i == 0)
        def _():
            for chip, source in enumerate((own, first_block, second_block, far_block)):
                left[chip * block : (chip + 1) * block, :] = source[...]

        def terms_of(gate, up):
            return contract_last(left[:, :half], gate) + contract_last(left[:, half:], up)

        @pl.when(i < 2)
        def _():
            terms = terms_of(own_gate[...], own_up[...])
            for q in range(members):
                for place in range(8):
                    at = place // 2 * block + (q * 2 + place % 2) * count
                    own_out[q, where[2 + place]] = terms[at : at + count]

        @pl.when(i >= 2)
        def _():
            terms = terms_of(other_gate[0], other_up[0]).astype(jnp.bfloat16)
            for q in range(members):
                for place in range(8):
                    at = place // 2 * block + (q * 2 + place % 2) * count
                    other_out[q, where[2 + place]] = terms[at : at + count]

    def first(i):
        return jnp.minimum(i, 1)

    def second(i):
        return jnp.maximum(i - 2, 0)

    own_weight = pl.BlockSpec((step, half), lambda i, where: (first(i), where[0]))
    other_weights = [
        pl.BlockSpec((1, step, half), lambda i, where, k=k: (k, second(i), 0)) for k in range(2)
    ]
    return steps.call(
        kernel,
        [
            jax.ShapeDtypeStruct((members, 8, count, width), jnp.float32),
            jax.ShapeDtypeStruct((members, 8, count, width), jnp.bfloat16),
        ],
        8 * rows * width * half,
        8 * width * half + 4 * rows * half + 6 * rows * width,
        (4,),
        [whole(x) for x in grads] + [own_weight] * 2 + other_weights,
        [
            pl.BlockSpec((members, 8, count, step), lambda i, where: (0, 0, 0, first(i))),
            pl.BlockSpec((members, 8, count, step), lambda i, where: (0, 0, 0, second(i))),
        ],
        grads + weights[:2] + [weights[2]] * 2,
        [pltpu.VMEM((rows, 2 * half), jnp.bfloat16)],
    )


def summed_terms(steps, own_terms, got):
    members, *rest = own_terms.shape

    def kernel(where, own_terms, got, *outs):
        for q in range(members):
            outs[q][...] = (own_terms[q] + got[q].astype(jnp.float32)).astype(jnp.bfloat16)

    return steps.call(
        kernel,
        [jax.ShapeDtypeStruct(rest, jnp.bfloat16)] * members,
        own_terms.size,
        8 * own_terms.size,
        (1,),
        [whole(own_terms), whole(got)],
        [pl.BlockSpec(rest, lambda i, where: (0, 0, 0))] * members,
        [own_terms, got],
    )


def chunk_steps(steps, chunk, here, saved, weights, downs):
    offsets, low, high = chunk
    if any(offsets):
        here = [arrived(steps, x) for x in here]
        yield
    there = [swap(x, "dp", 1) for x in here]
    send, keep = partial_sums(steps, chunk, here, there, *downs)
    got = exchange(send, 0)
    yield
    last = exchange(second_terms(steps, keep, got), 1)
    yield
    own = hidden_grads(steps, chunk, keep, got, last, saved)
    from_second, from_first = exchange(own, 1), exchange(own, 0)
    yield
    far = exchange(from_second, 0)
    steps.waits = steps.waits + [from_second]
    yield
    own_terms, other_terms = input_terms(steps, chunk, [own, from_first, from_second, far], weights)
    got = swap(other_terms, "dp", 1)
    yield
    terms = summed_terms(steps, own_terms, got)
    terms = [part if offset == 0 else swap(part, "et", offset) for offset, part in zip(offsets, terms)]
    yield
    steps.waits = steps.waits + terms
    yield terms


def per_device(out_grad, routes, gates, lengths, saved_gate, saved_up, w_gate, w_up, w_down):
    groups = lax.axis_size("dp")
    slots = saved_gate.shape[1] // lax.axis_size("et")
    width = w_gate.shape[0]
    me = lax.axis_index("dp")
    core = me % 2
    first, second = 2 + 2 * core, 4 - 2 * core
    place = [me ^ (chip + pair) for chip in (0, first, second, 6) for pair in (0, 1)]
    where = jnp.stack([core, lax.axis_index("et")] + place).astype(jnp.int32)

    downs = [w_down, swap(w_down, "dp", 1)]
    saved = [saved_gate, saved_up]
    weights = [w_gate, w_up]

    steps = Steps(where)
    rows, placing = packed_rows(steps, out_grad, routes.T, gates.T, lengths, groups, slots)
    rows = lax.all_to_all(rows, "dp", split_axis=0, concat_axis=0, tiled=True)
    sources = {
        offset: rows if offset == 0 else swap(rows, "et", offset)
        for offset in sorted({offset for offsets, _, _ in CHUNKS for offset in offsets})
    }
    chunks = [
        chunk_steps(steps, chunk, [sources[offset] for offset in chunk[0]], saved, weights, downs)
        for chunk in CHUNKS
    ]
    parts = {}
    steps.waits = [rows]
    for k in ORDER:
        if k < 0:
            other_weights, other_saved = other_halves(steps, weights, saved)
            weights.append(swap(other_weights, "dp", 1))
            saved.append(swap(other_saved, "dp", 1))
            continue
        for offset, part in zip(CHUNKS[k][0], next(chunks[k]) or []):
            parts.setdefault(offset, []).append(part)
    total = sum(jnp.concatenate(part, axis=1).astype(jnp.float32) for part in parts.values())
    summed = total.astype(jnp.bfloat16)
    summed = lax.all_to_all(summed, "dp", split_axis=0, concat_axis=1)
    summed = summed.reshape(slots, groups * width)
    input_grad = lax.dot_general(
        placing, summed, (((0,), (0,)), ((), ())), preferred_element_type=jnp.float32
    )
    return input_grad.astype(jnp.bfloat16)


def solution(mesh):
    in_specs = (
        P(("dp", "et"), None),
        P(("dp", "et"), None),
        P(("dp", "et"), None),
        P(("dp", "et"), None),
        P("dp", None, "et"),
        P("dp", None, "et"),
        P("dp", "et"),
        P("dp", "et"),
        P("et", "dp"),
    )
    out_specs = P(("dp", "et"), None)
    body = per_device if mesh.shape["dp"] == 8 and mesh.shape["et"] == 4 else plain_exchange
    return jax.shard_map(
        body, mesh=mesh, in_specs=in_specs, out_specs=out_specs, check_vma=False
    )
```

```python
import jax
import jax.numpy as jnp
from jax import lax
from jax.experimental import pallas as pl
from jax.experimental.pallas import tpu as pltpu
from jax.sharding import PartitionSpec as P


VMEM_LIMIT = 24 * 1024 * 1024
PACK_LIMIT = 60 * 1024 * 1024
CHUNKS = (((0,), 0, 32), ((2,), 0, 32), ((3,), 0, 32), ((1,), 0, 32))
SUM_STEPS = 2
ORDER = (0, 1, -1, 0, 1, 2, 0, 2, 0, 1, 3, 1, 2, 3, 1, 0, 2, 3, 0, 2, 3, 1, 0, 1, 3, 2, 1, 2, 3, 2, 3, 3)


def swiglu_grads(upstream, gate_pre, up_pre):
    gate_value = gate_pre.astype(jnp.float32)
    up_value = up_pre.astype(jnp.float32)
    sigmoid_gate = jax.nn.sigmoid(gate_value)
    slope = sigmoid_gate * (1.0 + gate_value * (1.0 - sigmoid_gate))
    grad_gate = (upstream * up_value * slope).astype(jnp.bfloat16)
    grad_up = (upstream * gate_value * sigmoid_gate).astype(jnp.bfloat16)
    return (grad_gate, grad_up)


def contract_last(left, right):
    axis = left.ndim - 1
    return lax.dot_general(
        left, right, (((axis,), (1,)), ((), ())), preferred_element_type=jnp.float32
    )


def place_rows(routes, gates, lengths, slots):
    tok_rows = routes.shape[0]
    hit_zero = routes == 0
    weight_zero = jnp.sum(jnp.where(hit_zero, gates, 0.0), axis=1)
    chosen = jnp.any(hit_zero, axis=1)
    doc_len = lengths[0]
    ends = jnp.cumsum(doc_len)
    starts = ends - doc_len
    position = jnp.arange(tok_rows, dtype=jnp.int32)
    inside = (position[:, None] >= starts[None, :]) & (position[:, None] < ends[None, :])
    mean_len = tok_rows / doc_len.shape[0]
    factor = jnp.sum(
        jnp.where(inside, mean_len / doc_len.astype(jnp.float32)[None, :], 0.0), axis=1
    )
    slot_of = jnp.cumsum(chosen.astype(jnp.int32)) - 1
    placing = (
        (slot_of[None, :] == jnp.arange(slots, dtype=jnp.int32)[:, None]) & chosen[None, :]
    ).astype(jnp.bfloat16)
    return placing, weight_zero * factor


def plain_exchange(out_grad, routes, gates, lengths, saved_gate, saved_up, w_gate, w_up, w_down):
    group_size = lax.axis_size("et")
    groups = lax.axis_size("dp")
    group_rows = saved_gate.shape[1]
    slots = group_rows // group_size
    width = w_gate.shape[0]
    placing, coef = place_rows(routes, gates, lengths, slots)
    scaled = (out_grad.astype(jnp.float32) * coef[:, None]).astype(jnp.bfloat16)
    packed = jnp.dot(placing, scaled, preferred_element_type=jnp.float32).astype(jnp.bfloat16)
    rows = lax.all_to_all(packed.reshape(slots, groups, width), "dp", split_axis=1, concat_axis=0)
    rows = rows.reshape(groups, slots, width)
    rows = lax.all_gather(rows, "et", axis=1)
    partial_up = contract_last(rows.reshape(groups * group_rows, width), w_down).astype(jnp.bfloat16)
    upstream = lax.psum_scatter(partial_up, "dp", scatter_dimension=0, tiled=True).astype(jnp.float32)
    grads = jnp.stack(swiglu_grads(upstream, saved_gate[0], saved_up[0]))
    grads = lax.all_gather(grads, "dp", axis=0)
    terms = contract_last(grads[:, 0], w_gate) + contract_last(grads[:, 1], w_up)
    terms = terms.astype(jnp.bfloat16).reshape(groups, group_size, slots, width)
    summed = lax.psum_scatter(terms, "et", scatter_dimension=1, tiled=False)
    summed = lax.all_to_all(summed, "dp", split_axis=0, concat_axis=1)
    summed = summed.reshape(slots, groups * width)
    input_grad = lax.dot_general(
        placing, summed, (((0,), (0,)), ((), ())), preferred_element_type=jnp.float32
    )
    return input_grad.astype(jnp.bfloat16)


def swap(values, axis, offset):
    size = lax.axis_size(axis)
    return lax.ppermute(values, axis, [(i, i ^ offset) for i in range(size)])


def exchange(values, turn):
    size = lax.axis_size("dp")
    return lax.ppermute(values, "dp", [(i, i ^ (2 if (i + turn) % 2 == 0 else 4)) for i in range(size)])


def whole(array):
    return pl.BlockSpec(array.shape, lambda i, where: (0,) * len(array.shape))


def shape(rows, columns, kind=jnp.bfloat16):
    return jax.ShapeDtypeStruct((rows, columns), kind)


class Steps:
    def __init__(self, where):
        self.where = where
        self.last = []
        self.waits = []

    def call(self, kernel, out_shape, flops, moved, grid, in_specs, out_specs, operands, scratch_shapes=(), limit=None, where=None):
        after = self.last + self.waits
        self.waits = []
        inputs = 1 + len(operands)

        def ordered(*refs):
            kernel(*refs[:inputs], *refs[inputs + len(after) :])

        results = pl.pallas_call(
            ordered,
            out_shape=out_shape,
            cost_estimate=pl.CostEstimate(flops=flops, bytes_accessed=moved, transcendentals=0),
            compiler_params=pltpu.CompilerParams(vmem_limit_bytes=limit or VMEM_LIMIT),
            grid_spec=pltpu.PrefetchScalarGridSpec(
                num_scalar_prefetch=1,
                grid=grid,
                in_specs=list(in_specs) + [pl.BlockSpec(memory_space=pl.ANY)] * len(after),
                out_specs=out_specs,
                scratch_shapes=scratch_shapes,
            ),
        )(self.where if where is None else where, *operands, *after)
        self.last = list(results[:1])
        return results


def whole(array):
    return pl.BlockSpec(array.shape, lambda i, where: (0,) * len(array.shape))


def shape(rows, columns, kind=jnp.bfloat16):
    return jax.ShapeDtypeStruct((rows, columns), kind)


def packed_rows(steps, out_grad, routes, gates, lengths, groups, slots):
    tokens, columns = out_grad.shape
    width = columns // groups
    documents = lengths.shape[1]
    strips = 2
    each = groups // strips

    def kernel(where, grad_ref, routes_ref, gates_ref, lengths_ref, rows_ref, placing_ref, coef_ref):
        @pl.when(pl.program_id(0) == 0)
        def _():
            hit_zero = routes_ref[...] == 0
            weight_zero = jnp.sum(jnp.where(hit_zero, gates_ref[...], 0.0), axis=0, keepdims=True)
            chosen = jnp.sum(jnp.where(hit_zero, 1.0, 0.0), axis=0, keepdims=True)
            position = lax.broadcasted_iota(jnp.int32, (1, tokens), 1)
            own_len = jnp.ones((1, tokens), jnp.float32)
            start = 0
            for document in range(documents):
                length = lengths_ref[0, document]
                inside = (position >= start) & (position < start + length)
                own_len = jnp.where(inside, length.astype(jnp.float32), own_len)
                start = start + length
            coef = weight_zero * ((tokens / documents) / own_len)
            token = lax.broadcasted_iota(jnp.int32, (tokens, tokens), 0)
            earlier = jnp.where(token <= lax.broadcasted_iota(jnp.int32, (tokens, tokens), 1), 1.0, 0.0).astype(jnp.bfloat16)
            counts = jnp.dot(
                jnp.broadcast_to(chosen, (slots, tokens)).astype(jnp.bfloat16),
                earlier,
                preferred_element_type=jnp.float32,
            )
            slot = lax.broadcasted_iota(jnp.int32, (slots, tokens), 0)
            taken = (counts.astype(jnp.int32) - 1 == slot) & (chosen > 0.0)
            placing_ref[...] = jnp.where(taken, 1.0, 0.0).astype(jnp.bfloat16)
            coef_ref[...] = jnp.sum(jnp.where(taken, coef, 0.0), axis=1, keepdims=True)

        rows = jnp.dot(placing_ref[...], grad_ref[...], preferred_element_type=jnp.float32)
        rows = (rows * coef_ref[...]).astype(jnp.bfloat16)
        for k in range(each):
            rows_ref[k] = rows[:, k * width : (k + 1) * width]

    return steps.call(
        kernel,
        [jax.ShapeDtypeStruct((groups, slots, width), jnp.bfloat16), shape(slots, tokens)],
        2 * tokens * slots * columns,
        2 * tokens * columns + 2 * slots * columns,
        (strips,),
        [
            pl.BlockSpec((tokens, columns // strips), lambda i, where: (0, i)),
            whole(routes),
            whole(gates),
            pl.BlockSpec(memory_space=pltpu.SMEM),
        ],
        [
            pl.BlockSpec((each, slots, width), lambda i, where: (i, 0, 0)),
            pl.BlockSpec((slots, tokens), lambda i, where: (0, 0)),
        ],
        [out_grad, routes, gates, lengths],
        [pltpu.VMEM((slots, 1), jnp.float32)],
        PACK_LIMIT,
        jnp.zeros((1,), jnp.int32),
    )


def other_halves(steps, weights, saved):
    width, hidden = weights[0].shape
    rows = saved[0].shape[1]
    half = hidden // 2
    parts = 4

    def kernel(where, gate, up, saved_gate, saved_up, weights_out, saved_out):
        weights_out[0], weights_out[1] = gate[...], up[...]
        saved_out[0], saved_out[1] = saved_gate[0], saved_up[0]

    return steps.call(
        kernel,
        [
            jax.ShapeDtypeStruct((2, width, half), jnp.bfloat16),
            jax.ShapeDtypeStruct((2, rows, half), jnp.bfloat16),
        ],
        0,
        8 * (width + rows) * half,
        (parts,),
        [pl.BlockSpec((width // parts, half), lambda i, where: (i, 1 - where[0]))] * 2
        + [pl.BlockSpec((1, rows // parts, half), lambda i, where: (0, i, 1 - where[0]))] * 2,
        [
            pl.BlockSpec((2, width // parts, half), lambda i, where: (0, i, 0)),
            pl.BlockSpec((2, rows // parts, half), lambda i, where: (0, i, 0)),
        ],
        weights + saved,
    )


def arrived(steps, rows):
    def kernel(where, rows, out):
        out[...] = rows[...]

    return steps.call(
        kernel,
        [jax.ShapeDtypeStruct(rows.shape, rows.dtype)],
        0,
        4 * rows.size,
        (1,),
        [whole(rows)],
        [whole(rows)],
        [rows],
    )[0]


def partial_sums(steps, chunk, here, there, own_down, other_down):
    offsets, low, high = chunk
    members, count = len(offsets), high - low
    width = own_down.shape[1]
    block = members * 2 * count
    half = own_down.shape[0] // 2
    step = half // SUM_STEPS

    def kernel(where, *refs):
        own_ref, other_ref, send, keep, left = refs[2 * members :]

        @pl.when(pl.program_id(0) == 0)
        def _():
            for q in range(members):
                for place in range(8):
                    to = place // 2 * block + (q * 2 + place % 2) * count
                    group = where[2 + place]
                    left[to : to + count, :width] = refs[q][group, low:high, :]
                    left[to : to + count, width:] = refs[members + q][group, low:high, :]

        sums = contract_last(left[:, :width], own_ref[...]) + contract_last(left[:, width:], other_ref[...])
        sums = sums.astype(jnp.bfloat16)
        keep[:block], send[:block] = sums[:block], sums[block : 2 * block]
        keep[block:], send[block:] = sums[2 * block : 3 * block], sums[3 * block :]

    weight = pl.BlockSpec((step, width), lambda i, where: (where[0] * SUM_STEPS + i, 0))
    return steps.call(
        kernel,
        [shape(2 * block, half)] * 2,
        16 * block * width * half,
        4 * half * width + 8 * block * (2 * width + half),
        (SUM_STEPS,),
        [whole(x) for x in here + there] + [weight, weight],
        [pl.BlockSpec((2 * block, step), lambda i, where: (0, i))] * 2,
        here + there + [own_down, other_down],
        [pltpu.VMEM((4 * block, 2 * width), jnp.bfloat16)],
    )


def second_terms(steps, keep, got):
    rows, columns = keep.shape[0] // 2, keep.shape[1]

    def kernel(where, keep, got, send):
        send[...] = (keep[...].astype(jnp.float32) + got[...].astype(jnp.float32)).astype(jnp.bfloat16)

    return steps.call(
        kernel,
        [shape(rows, columns)],
        rows * columns,
        6 * rows * columns,
        (1,),
        [pl.BlockSpec((rows, columns), lambda i, where: (1, 0))] * 2,
        [pl.BlockSpec((rows, columns), lambda i, where: (0, 0))],
        [keep, got],
    )[0]


def hidden_grads(steps, chunk, keep, got, last, saved):
    offsets, low, high = chunk
    members, count = len(offsets), high - low
    rows, columns = last.shape

    def kernel(where, keep, got, last, *refs):
        out = refs[-1]
        for q in range(members):
            for core in range(2):
                take = pl.ds((q * 2 + core) * count, count)
                upstream = (
                    keep[take, :].astype(jnp.float32)
                    + got[take, :].astype(jnp.float32)
                    + last[take, :].astype(jnp.float32)
                )
                gate, up = refs[(q * 2 + core) * 2 : (q * 2 + core) * 2 + 2]
                grad_gate, grad_up = swiglu_grads(upstream, gate[0], up[0])
                out[take, :columns] = grad_gate
                out[take, columns:] = grad_up

    upper = pl.BlockSpec((rows, columns), lambda i, where: (0, 0))
    slots = saved[0].shape[1] // lax.axis_size("et")

    def row(where, offset):
        return ((where[1] ^ offset) * slots + low) // count

    def own_spec(offset):
        return pl.BlockSpec((1, count, columns), lambda i, where: (0, row(where, offset), where[0]))

    def other_spec(offset, which):
        return pl.BlockSpec((1, count, columns), lambda i, where: (which, row(where, offset), 0))

    saved_specs = [
        spec for offset in offsets for spec in [own_spec(offset)] * 2 + [other_spec(offset, k) for k in range(2)]
    ]
    return steps.call(
        kernel,
        [shape(rows, 2 * columns)],
        40 * rows * columns,
        14 * rows * columns,
        (1,),
        [upper] * 3 + saved_specs,
        [pl.BlockSpec((rows, 2 * columns), lambda i, where: (0, 0))],
        [keep, got, last] + (saved[:2] + [saved[2]] * 2) * members,
    )[0]


def input_terms(steps, chunk, grads, weights):
    offsets, low, high = chunk
    members, count = len(offsets), high - low
    block, half = grads[0].shape[0], grads[0].shape[1] // 2
    rows = 4 * block
    width = weights[0].shape[0]
    step = width // 2

    def kernel(where, own, first_block, second_block, far_block, own_gate, own_up, other_gate, other_up, *refs):
        own_out, other_out, left = refs
        i = pl.program_id(0)

        @pl.when(i == 0)
        def _():
            for chip, source in enumerate((own, first_block, second_block, far_block)):
                left[chip * block : (chip + 1) * block, :] = source[...]

        def terms_of(gate, up):
            return contract_last(left[:, :half], gate) + contract_last(left[:, half:], up)

        @pl.when(i < 2)
        def _():
            terms = terms_of(own_gate[...], own_up[...])
            for q in range(members):
                for place in range(8):
                    at = place // 2 * block + (q * 2 + place % 2) * count
                    own_out[q, where[2 + place]] = terms[at : at + count]

        @pl.when(i >= 2)
        def _():
            terms = terms_of(other_gate[0], other_up[0]).astype(jnp.bfloat16)
            for q in range(members):
                for place in range(8):
                    at = place // 2 * block + (q * 2 + place % 2) * count
                    other_out[q, where[2 + place]] = terms[at : at + count]

    def first(i):
        return jnp.minimum(i, 1)

    def second(i):
        return jnp.maximum(i - 2, 0)

    own_weight = pl.BlockSpec((step, half), lambda i, where: (first(i), where[0]))
    other_weights = [
        pl.BlockSpec((1, step, half), lambda i, where, k=k: (k, second(i), 0)) for k in range(2)
    ]
    return steps.call(
        kernel,
        [
            jax.ShapeDtypeStruct((members, 8, count, width), jnp.float32),
            jax.ShapeDtypeStruct((members, 8, count, width), jnp.bfloat16),
        ],
        8 * rows * width * half,
        8 * width * half + 4 * rows * half + 6 * rows * width,
        (4,),
        [whole(x) for x in grads] + [own_weight] * 2 + other_weights,
        [
            pl.BlockSpec((members, 8, count, step), lambda i, where: (0, 0, 0, first(i))),
            pl.BlockSpec((members, 8, count, step), lambda i, where: (0, 0, 0, second(i))),
        ],
        grads + weights[:2] + [weights[2]] * 2,
        [pltpu.VMEM((rows, 2 * half), jnp.bfloat16)],
    )


def summed_terms(steps, own_terms, got):
    members, *rest = own_terms.shape

    def kernel(where, own_terms, got, *outs):
        for q in range(members):
            outs[q][...] = (own_terms[q] + got[q].astype(jnp.float32)).astype(jnp.bfloat16)

    return steps.call(
        kernel,
        [jax.ShapeDtypeStruct(rest, jnp.bfloat16)] * members,
        own_terms.size,
        8 * own_terms.size,
        (1,),
        [whole(own_terms), whole(got)],
        [pl.BlockSpec(rest, lambda i, where: (0, 0, 0))] * members,
        [own_terms, got],
    )


def chunk_steps(steps, chunk, here, saved, weights, downs):
    offsets, low, high = chunk
    if any(offsets):
        here = [arrived(steps, x) for x in here]
        yield
    there = [swap(x, "dp", 1) for x in here]
    send, keep = partial_sums(steps, chunk, here, there, *downs)
    got = exchange(send, 0)
    yield
    last = exchange(second_terms(steps, keep, got), 1)
    yield
    own = hidden_grads(steps, chunk, keep, got, last, saved)
    from_second, from_first = exchange(own, 1), exchange(own, 0)
    yield
    far = exchange(from_second, 0)
    steps.waits = steps.waits + [from_second]
    yield
    own_terms, other_terms = input_terms(steps, chunk, [own, from_first, from_second, far], weights)
    got = swap(other_terms, "dp", 1)
    yield
    terms = summed_terms(steps, own_terms, got)
    terms = [part if offset == 0 else swap(part, "et", offset) for offset, part in zip(offsets, terms)]
    yield
    steps.waits = steps.waits + terms
    yield terms


def per_device(out_grad, routes, gates, lengths, saved_gate, saved_up, w_gate, w_up, w_down):
    groups = lax.axis_size("dp")
    slots = saved_gate.shape[1] // lax.axis_size("et")
    width = w_gate.shape[0]
    me = lax.axis_index("dp")
    core = me % 2
    first, second = 2 + 2 * core, 4 - 2 * core
    place = [me ^ (chip + pair) for chip in (0, first, second, 6) for pair in (0, 1)]
    where = jnp.stack([core, lax.axis_index("et")] + place).astype(jnp.int32)

    downs = [w_down, swap(w_down, "dp", 1)]
    saved = [saved_gate, saved_up]
    weights = [w_gate, w_up]

    steps = Steps(where)
    rows, placing = packed_rows(steps, out_grad, routes.T, gates.T, lengths, groups, slots)
    rows = lax.all_to_all(rows, "dp", split_axis=0, concat_axis=0, tiled=True)
    sources = {
        offset: rows if offset == 0 else swap(rows, "et", offset)
        for offset in sorted({offset for offsets, _, _ in CHUNKS for offset in offsets})
    }
    chunks = [
        chunk_steps(steps, chunk, [sources[offset] for offset in chunk[0]], saved, weights, downs)
        for chunk in CHUNKS
    ]
    parts = {}
    steps.waits = [rows]
    for k in ORDER:
        if k < 0:
            other_weights, other_saved = other_halves(steps, weights, saved)
            weights.append(swap(other_weights, "dp", 1))
            saved.append(swap(other_saved, "dp", 1))
            continue
        for offset, part in zip(CHUNKS[k][0], next(chunks[k]) or []):
            parts.setdefault(offset, []).append(part)
    total = sum(jnp.concatenate(part, axis=1).astype(jnp.float32) for part in parts.values())
    summed = total.astype(jnp.bfloat16)
    summed = lax.all_to_all(summed, "dp", split_axis=0, concat_axis=1)
    summed = summed.reshape(slots, groups * width)
    input_grad = lax.dot_general(
        placing, summed, (((0,), (0,)), ((), ())), preferred_element_type=jnp.float32
    )
    return input_grad.astype(jnp.bfloat16)


def solution(mesh):
    in_specs = (
        P(("dp", "et"), None),
        P(("dp", "et"), None),
        P(("dp", "et"), None),
        P(("dp", "et"), None),
        P("dp", None, "et"),
        P("dp", None, "et"),
        P("dp", "et"),
        P("dp", "et"),
        P("et", "dp"),
    )
    out_specs = P(("dp", "et"), None)
    body = per_device if mesh.shape["dp"] == 8 and mesh.shape["et"] == 4 else plain_exchange
    return jax.shard_map(
        body, mesh=mesh, in_specs=in_specs, out_specs=out_specs, check_vma=False
    )
```

```python
import jax
import jax.numpy as jnp
from jax import lax
from jax.experimental import pallas as pl
from jax.experimental.pallas import tpu as pltpu
from jax.sharding import PartitionSpec as P


VMEM_LIMIT = 24 * 1024 * 1024
PACK_LIMIT = 60 * 1024 * 1024
CHUNKS = (((0,), 0, 32), ((2,), 0, 32), ((3,), 0, 32), ((1,), 0, 32))
SUM_STEPS = 2
ORDER = (0, 1, -1, 0, 1, 2, 0, 2, 0, 1, 3, 1, 2, 3, 1, 0, 2, 3, 0, 2, 3, 1, 0, 1, 3, 2, 1, 2, 3, 2, 3, 3)


def swiglu_grads(upstream, gate_pre, up_pre):
    gate_value = gate_pre.astype(jnp.float32)
    up_value = up_pre.astype(jnp.float32)
    sigmoid_gate = jax.nn.sigmoid(gate_value)
    slope = sigmoid_gate * (1.0 + gate_value * (1.0 - sigmoid_gate))
    grad_gate = (upstream * up_value * slope).astype(jnp.bfloat16)
    grad_up = (upstream * gate_value * sigmoid_gate).astype(jnp.bfloat16)
    return (grad_gate, grad_up)


def contract_last(left, right):
    axis = left.ndim - 1
    return lax.dot_general(
        left, right, (((axis,), (1,)), ((), ())), preferred_element_type=jnp.float32
    )


def place_rows(routes, gates, lengths, slots):
    tok_rows = routes.shape[0]
    hit_zero = routes == 0
    weight_zero = jnp.sum(jnp.where(hit_zero, gates, 0.0), axis=1)
    chosen = jnp.any(hit_zero, axis=1)
    doc_len = lengths[0]
    ends = jnp.cumsum(doc_len)
    starts = ends - doc_len
    position = jnp.arange(tok_rows, dtype=jnp.int32)
    inside = (position[:, None] >= starts[None, :]) & (position[:, None] < ends[None, :])
    mean_len = tok_rows / doc_len.shape[0]
    factor = jnp.sum(
        jnp.where(inside, mean_len / doc_len.astype(jnp.float32)[None, :], 0.0), axis=1
    )
    slot_of = jnp.cumsum(chosen.astype(jnp.int32)) - 1
    placing = (
        (slot_of[None, :] == jnp.arange(slots, dtype=jnp.int32)[:, None]) & chosen[None, :]
    ).astype(jnp.bfloat16)
    return placing, weight_zero * factor


def plain_exchange(out_grad, routes, gates, lengths, saved_gate, saved_up, w_gate, w_up, w_down):
    group_size = lax.axis_size("et")
    groups = lax.axis_size("dp")
    group_rows = saved_gate.shape[1]
    slots = group_rows // group_size
    width = w_gate.shape[0]
    placing, coef = place_rows(routes, gates, lengths, slots)
    scaled = (out_grad.astype(jnp.float32) * coef[:, None]).astype(jnp.bfloat16)
    packed = jnp.dot(placing, scaled, preferred_element_type=jnp.float32).astype(jnp.bfloat16)
    rows = lax.all_to_all(packed.reshape(slots, groups, width), "dp", split_axis=1, concat_axis=0)
    rows = rows.reshape(groups, slots, width)
    rows = lax.all_gather(rows, "et", axis=1)
    partial_up = contract_last(rows.reshape(groups * group_rows, width), w_down).astype(jnp.bfloat16)
    upstream = lax.psum_scatter(partial_up, "dp", scatter_dimension=0, tiled=True).astype(jnp.float32)
    grads = jnp.stack(swiglu_grads(upstream, saved_gate[0], saved_up[0]))
    grads = lax.all_gather(grads, "dp", axis=0)
    terms = contract_last(grads[:, 0], w_gate) + contract_last(grads[:, 1], w_up)
    terms = terms.astype(jnp.bfloat16).reshape(groups, group_size, slots, width)
    summed = lax.psum_scatter(terms, "et", scatter_dimension=1, tiled=False)
    summed = lax.all_to_all(summed, "dp", split_axis=0, concat_axis=1)
    summed = summed.reshape(slots, groups * width)
    input_grad = lax.dot_general(
        placing, summed, (((0,), (0,)), ((), ())), preferred_element_type=jnp.float32
    )
    return input_grad.astype(jnp.bfloat16)


def swap(values, axis, offset):
    size = lax.axis_size(axis)
    return lax.ppermute(values, axis, [(i, i ^ offset) for i in range(size)])


def exchange(values, turn):
    size = lax.axis_size("dp")
    return lax.ppermute(values, "dp", [(i, i ^ (2 if (i + turn) % 2 == 0 else 4)) for i in range(size)])


def whole(array):
    return pl.BlockSpec(array.shape, lambda i, where: (0,) * len(array.shape))


def shape(rows, columns, kind=jnp.bfloat16):
    return jax.ShapeDtypeStruct((rows, columns), kind)


class Steps:
    def __init__(self, where):
        self.where = where
        self.last = []
        self.waits = []

    def call(self, kernel, out_shape, flops, moved, grid, in_specs, out_specs, operands, scratch_shapes=(), limit=None, where=None):
        after = self.last + self.waits
        self.waits = []
        inputs = 1 + len(operands)

        def ordered(*refs):
            kernel(*refs[:inputs], *refs[inputs + len(after) :])

        results = pl.pallas_call(
            ordered,
            out_shape=out_shape,
            cost_estimate=pl.CostEstimate(flops=flops, bytes_accessed=moved, transcendentals=0),
            compiler_params=pltpu.CompilerParams(vmem_limit_bytes=limit or VMEM_LIMIT),
            grid_spec=pltpu.PrefetchScalarGridSpec(
                num_scalar_prefetch=1,
                grid=grid,
                in_specs=list(in_specs) + [pl.BlockSpec(memory_space=pl.ANY)] * len(after),
                out_specs=out_specs,
                scratch_shapes=scratch_shapes,
            ),
        )(self.where if where is None else where, *operands, *after)
        self.last = list(results[:1])
        return results


def whole(array):
    return pl.BlockSpec(array.shape, lambda i, where: (0,) * len(array.shape))


def shape(rows, columns, kind=jnp.bfloat16):
    return jax.ShapeDtypeStruct((rows, columns), kind)


def packed_rows(steps, out_grad, routes, gates, lengths, groups, slots):
    tokens, columns = out_grad.shape
    width = columns // groups
    documents = lengths.shape[1]
    strips = 2
    each = groups // strips

    def kernel(where, grad_ref, routes_ref, gates_ref, lengths_ref, rows_ref, placing_ref, coef_ref):
        @pl.when(pl.program_id(0) == 0)
        def _():
            hit_zero = routes_ref[...] == 0
            weight_zero = jnp.sum(jnp.where(hit_zero, gates_ref[...], 0.0), axis=0, keepdims=True)
            chosen = jnp.sum(jnp.where(hit_zero, 1.0, 0.0), axis=0, keepdims=True)
            position = lax.broadcasted_iota(jnp.int32, (1, tokens), 1)
            own_len = jnp.ones((1, tokens), jnp.float32)
            start = 0
            for document in range(documents):
                length = lengths_ref[0, document]
                inside = (position >= start) & (position < start + length)
                own_len = jnp.where(inside, length.astype(jnp.float32), own_len)
                start = start + length
            coef = weight_zero * ((tokens / documents) / own_len)
            token = lax.broadcasted_iota(jnp.int32, (tokens, tokens), 0)
            earlier = jnp.where(token <= lax.broadcasted_iota(jnp.int32, (tokens, tokens), 1), 1.0, 0.0).astype(jnp.bfloat16)
            counts = jnp.dot(
                jnp.broadcast_to(chosen, (slots, tokens)).astype(jnp.bfloat16),
                earlier,
                preferred_element_type=jnp.float32,
            )
            slot = lax.broadcasted_iota(jnp.int32, (slots, tokens), 0)
            taken = (counts.astype(jnp.int32) - 1 == slot) & (chosen > 0.0)
            placing_ref[...] = jnp.where(taken, 1.0, 0.0).astype(jnp.bfloat16)
            coef_ref[...] = jnp.sum(jnp.where(taken, coef, 0.0), axis=1, keepdims=True)

        rows = jnp.dot(placing_ref[...], grad_ref[...], preferred_element_type=jnp.float32)
        rows = (rows * coef_ref[...]).astype(jnp.bfloat16)
        for k in range(each):
            rows_ref[k] = rows[:, k * width : (k + 1) * width]

    return steps.call(
        kernel,
        [jax.ShapeDtypeStruct((groups, slots, width), jnp.bfloat16), shape(slots, tokens)],
        2 * tokens * slots * columns,
        2 * tokens * columns + 2 * slots * columns,
        (strips,),
        [
            pl.BlockSpec((tokens, columns // strips), lambda i, where: (0, i)),
            whole(routes),
            whole(gates),
            pl.BlockSpec(memory_space=pltpu.SMEM),
        ],
        [
            pl.BlockSpec((each, slots, width), lambda i, where: (i, 0, 0)),
            pl.BlockSpec((slots, tokens), lambda i, where: (0, 0)),
        ],
        [out_grad, routes, gates, lengths],
        [pltpu.VMEM((slots, 1), jnp.float32)],
        PACK_LIMIT,
        jnp.zeros((1,), jnp.int32),
    )


def other_halves(steps, weights, saved):
    width, hidden = weights[0].shape
    rows = saved[0].shape[1]
    half = hidden // 2
    parts = 4

    def kernel(where, gate, up, saved_gate, saved_up, weights_out, saved_out):
        weights_out[0], weights_out[1] = gate[...], up[...]
        saved_out[0], saved_out[1] = saved_gate[0], saved_up[0]

    return steps.call(
        kernel,
        [
            jax.ShapeDtypeStruct((2, width, half), jnp.bfloat16),
            jax.ShapeDtypeStruct((2, rows, half), jnp.bfloat16),
        ],
        0,
        8 * (width + rows) * half,
        (parts,),
        [pl.BlockSpec((width // parts, half), lambda i, where: (i, 1 - where[0]))] * 2
        + [pl.BlockSpec((1, rows // parts, half), lambda i, where: (0, i, 1 - where[0]))] * 2,
        [
            pl.BlockSpec((2, width // parts, half), lambda i, where: (0, i, 0)),
            pl.BlockSpec((2, rows // parts, half), lambda i, where: (0, i, 0)),
        ],
        weights + saved,
    )


def arrived(steps, rows):
    def kernel(where, rows, out):
        out[...] = rows[...]

    return steps.call(
        kernel,
        [jax.ShapeDtypeStruct(rows.shape, rows.dtype)],
        0,
        4 * rows.size,
        (1,),
        [whole(rows)],
        [whole(rows)],
        [rows],
    )[0]


def partial_sums(steps, chunk, here, there, own_down, other_down):
    offsets, low, high = chunk
    members, count = len(offsets), high - low
    width = own_down.shape[1]
    block = members * 2 * count
    half = own_down.shape[0] // 2
    step = half // SUM_STEPS

    def kernel(where, *refs):
        own_ref, other_ref, send, keep, left = refs[2 * members :]

        @pl.when(pl.program_id(0) == 0)
        def _():
            for q in range(members):
                for place in range(8):
                    to = place // 2 * block + (q * 2 + place % 2) * count
                    group = where[2 + place]
                    left[to : to + count, :width] = refs[q][group, low:high, :]
                    left[to : to + count, width:] = refs[members + q][group, low:high, :]

        sums = contract_last(left[:, :width], own_ref[...]) + contract_last(left[:, width:], other_ref[...])
        sums = sums.astype(jnp.bfloat16)
        keep[:block], send[:block] = sums[:block], sums[block : 2 * block]
        keep[block:], send[block:] = sums[2 * block : 3 * block], sums[3 * block :]

    weight = pl.BlockSpec((step, width), lambda i, where: (where[0] * SUM_STEPS + i, 0))
    return steps.call(
        kernel,
        [shape(2 * block, half)] * 2,
        16 * block * width * half,
        4 * half * width + 8 * block * (2 * width + half),
        (SUM_STEPS,),
        [whole(x) for x in here + there] + [weight, weight],
        [pl.BlockSpec((2 * block, step), lambda i, where: (0, i))] * 2,
        here + there + [own_down, other_down],
        [pltpu.VMEM((4 * block, 2 * width), jnp.bfloat16)],
    )


def second_terms(steps, keep, got):
    rows, columns = keep.shape[0] // 2, keep.shape[1]

    def kernel(where, keep, got, send):
        send[...] = (keep[...].astype(jnp.float32) + got[...].astype(jnp.float32)).astype(jnp.bfloat16)

    return steps.call(
        kernel,
        [shape(rows, columns)],
        rows * columns,
        6 * rows * columns,
        (1,),
        [pl.BlockSpec((rows, columns), lambda i, where: (1, 0))] * 2,
        [pl.BlockSpec((rows, columns), lambda i, where: (0, 0))],
        [keep, got],
    )[0]


def hidden_grads(steps, chunk, keep, got, last, saved):
    offsets, low, high = chunk
    members, count = len(offsets), high - low
    rows, columns = last.shape

    def kernel(where, keep, got, last, *refs):
        out = refs[-1]
        for q in range(members):
            for core in range(2):
                take = pl.ds((q * 2 + core) * count, count)
                upstream = (
                    keep[take, :].astype(jnp.float32)
                    + got[take, :].astype(jnp.float32)
                    + last[take, :].astype(jnp.float32)
                )
                gate, up = refs[(q * 2 + core) * 2 : (q * 2 + core) * 2 + 2]
                grad_gate, grad_up = swiglu_grads(upstream, gate[0], up[0])
                out[take, :columns] = grad_gate
                out[take, columns:] = grad_up

    upper = pl.BlockSpec((rows, columns), lambda i, where: (0, 0))
    slots = saved[0].shape[1] // lax.axis_size("et")

    def row(where, offset):
        return ((where[1] ^ offset) * slots + low) // count

    def own_spec(offset):
        return pl.BlockSpec((1, count, columns), lambda i, where: (0, row(where, offset), where[0]))

    def other_spec(offset, which):
        return pl.BlockSpec((1, count, columns), lambda i, where: (which, row(where, offset), 0))

    saved_specs = [
        spec for offset in offsets for spec in [own_spec(offset)] * 2 + [other_spec(offset, k) for k in range(2)]
    ]
    return steps.call(
        kernel,
        [shape(rows, 2 * columns)],
        40 * rows * columns,
        14 * rows * columns,
        (1,),
        [upper] * 3 + saved_specs,
        [pl.BlockSpec((rows, 2 * columns), lambda i, where: (0, 0))],
        [keep, got, last] + (saved[:2] + [saved[2]] * 2) * members,
    )[0]


def input_terms(steps, chunk, grads, weights):
    offsets, low, high = chunk
    members, count = len(offsets), high - low
    block, half = grads[0].shape[0], grads[0].shape[1] // 2
    rows = 4 * block
    width = weights[0].shape[0]
    step = width // 2

    def kernel(where, own, first_block, second_block, far_block, own_gate, own_up, other_gate, other_up, *refs):
        own_out, other_out, left = refs
        i = pl.program_id(0)

        @pl.when(i == 0)
        def _():
            for chip, source in enumerate((own, first_block, second_block, far_block)):
                left[chip * block : (chip + 1) * block, :] = source[...]

        def terms_of(gate, up):
            return contract_last(left[:, :half], gate) + contract_last(left[:, half:], up)

        @pl.when(i < 2)
        def _():
            terms = terms_of(own_gate[...], own_up[...])
            for q in range(members):
                for place in range(8):
                    at = place // 2 * block + (q * 2 + place % 2) * count
                    own_out[q, where[2 + place]] = terms[at : at + count]

        @pl.when(i >= 2)
        def _():
            terms = terms_of(other_gate[0], other_up[0]).astype(jnp.bfloat16)
            for q in range(members):
                for place in range(8):
                    at = place // 2 * block + (q * 2 + place % 2) * count
                    other_out[q, where[2 + place]] = terms[at : at + count]

    def first(i):
        return jnp.minimum(i, 1)

    def second(i):
        return jnp.maximum(i - 2, 0)

    own_weight = pl.BlockSpec((step, half), lambda i, where: (first(i), where[0]))
    other_weights = [
        pl.BlockSpec((1, step, half), lambda i, where, k=k: (k, second(i), 0)) for k in range(2)
    ]
    return steps.call(
        kernel,
        [
            jax.ShapeDtypeStruct((members, 8, count, width), jnp.float32),
            jax.ShapeDtypeStruct((members, 8, count, width), jnp.bfloat16),
        ],
        8 * rows * width * half,
        8 * width * half + 4 * rows * half + 6 * rows * width,
        (4,),
        [whole(x) for x in grads] + [own_weight] * 2 + other_weights,
        [
            pl.BlockSpec((members, 8, count, step), lambda i, where: (0, 0, 0, first(i))),
            pl.BlockSpec((members, 8, count, step), lambda i, where: (0, 0, 0, second(i))),
        ],
        grads + weights[:2] + [weights[2]] * 2,
        [pltpu.VMEM((rows, 2 * half), jnp.bfloat16)],
    )


def summed_terms(steps, own_terms, got):
    members, *rest = own_terms.shape

    def kernel(where, own_terms, got, *outs):
        for q in range(members):
            outs[q][...] = (own_terms[q] + got[q].astype(jnp.float32)).astype(jnp.bfloat16)

    return steps.call(
        kernel,
        [jax.ShapeDtypeStruct(rest, jnp.bfloat16)] * members,
        own_terms.size,
        8 * own_terms.size,
        (1,),
        [whole(own_terms), whole(got)],
        [pl.BlockSpec(rest, lambda i, where: (0, 0, 0))] * members,
        [own_terms, got],
    )


def chunk_steps(steps, chunk, here, saved, weights, downs):
    offsets, low, high = chunk
    if any(offsets):
        here = [arrived(steps, x) for x in here]
        yield
    there = [swap(x, "dp", 1) for x in here]
    send, keep = partial_sums(steps, chunk, here, there, *downs)
    got = exchange(send, 0)
    yield
    last = exchange(second_terms(steps, keep, got), 1)
    yield
    own = hidden_grads(steps, chunk, keep, got, last, saved)
    from_second = exchange(own, 1)
    yield
    far, from_first = exchange(from_second, 0), exchange(own, 0)
    steps.waits = steps.waits + [from_second]
    yield
    own_terms, other_terms = input_terms(steps, chunk, [own, from_first, from_second, far], weights)
    got = swap(other_terms, "dp", 1)
    yield
    terms = summed_terms(steps, own_terms, got)
    terms = [part if offset == 0 else swap(part, "et", offset) for offset, part in zip(offsets, terms)]
    yield
    steps.waits = steps.waits + terms
    yield terms


def per_device(out_grad, routes, gates, lengths, saved_gate, saved_up, w_gate, w_up, w_down):
    groups = lax.axis_size("dp")
    slots = saved_gate.shape[1] // lax.axis_size("et")
    width = w_gate.shape[0]
    me = lax.axis_index("dp")
    core = me % 2
    first, second = 2 + 2 * core, 4 - 2 * core
    place = [me ^ (chip + pair) for chip in (0, first, second, 6) for pair in (0, 1)]
    where = jnp.stack([core, lax.axis_index("et")] + place).astype(jnp.int32)

    downs = [w_down, swap(w_down, "dp", 1)]
    saved = [saved_gate, saved_up]
    weights = [w_gate, w_up]

    steps = Steps(where)
    rows, placing = packed_rows(steps, out_grad, routes.T, gates.T, lengths, groups, slots)
    rows = lax.all_to_all(rows, "dp", split_axis=0, concat_axis=0, tiled=True)
    sources = {
        offset: rows if offset == 0 else swap(rows, "et", offset)
        for offset in sorted({offset for offsets, _, _ in CHUNKS for offset in offsets})
    }
    chunks = [
        chunk_steps(steps, chunk, [sources[offset] for offset in chunk[0]], saved, weights, downs)
        for chunk in CHUNKS
    ]
    parts = {}
    steps.waits = [rows]
    for k in ORDER:
        if k < 0:
            other_weights, other_saved = other_halves(steps, weights, saved)
            weights.append(swap(other_weights, "dp", 1))
            saved.append(swap(other_saved, "dp", 1))
            continue
        for offset, part in zip(CHUNKS[k][0], next(chunks[k]) or []):
            parts.setdefault(offset, []).append(part)
    total = sum(jnp.concatenate(part, axis=1).astype(jnp.float32) for part in parts.values())
    summed = total.astype(jnp.bfloat16)
    summed = lax.all_to_all(summed, "dp", split_axis=0, concat_axis=1)
    summed = summed.reshape(slots, groups * width)
    input_grad = lax.dot_general(
        placing, summed, (((0,), (0,)), ((), ())), preferred_element_type=jnp.float32
    )
    return input_grad.astype(jnp.bfloat16)


def solution(mesh):
    in_specs = (
        P(("dp", "et"), None),
        P(("dp", "et"), None),
        P(("dp", "et"), None),
        P(("dp", "et"), None),
        P("dp", None, "et"),
        P("dp", None, "et"),
        P("dp", "et"),
        P("dp", "et"),
        P("et", "dp"),
    )
    out_specs = P(("dp", "et"), None)
    body = per_device if mesh.shape["dp"] == 8 and mesh.shape["et"] == 4 else plain_exchange
    return jax.shard_map(
        body, mesh=mesh, in_specs=in_specs, out_specs=out_specs, check_vma=False
    )
```
